32 devices in a mesh: wide: 8 (over z, y), narrow: 4 (over x, core).
Axes of the slice: x: 2, y: 2, z: 4, core: 2. Of those that a mesh axis runs over, the one named last changes fastest.
Arguments:
- target_slot: int32 [1024], replicated, may hold values from 0 to 1023, as said below
- fields: bfloat16 [1024, 8, 4096], P(('wide', 'narrow')), as said below
Outputs:
- migrated: bfloat16 [1024, 8, 4096], P(('wide', 'narrow'))
- pressure: float32 [64, 512, 128], P('narrow', 'wide')
The draws below stay inside these ranges and needn't reach their ends.
Inputs may be any that keep to these rules, and one draw needn't show every extreme that they name: `target_slot`: A permutation of the patches. Owner w * 4 + n holds patches w * 4 + n times 32 onward, old and new. From one owner to any owner go at most 2 patches, and exactly 2 for some pairs in every draw; every owner receives exactly 32 patches. `fields`: fields 0, 1, 2 are velocity components along the three dimensions, field 3 is the density, between 0.6 and 8.1; the others are carried quantities.
All inputs are finite; a program needn't handle non-finite values.
Results may differ from the reference program's by a relative error of at most 0.0014.
Values may be sent and summed in bfloat16 or wider, within the bound.
A program may use at most 128 MiB of HBM per device.

```python
import jax
import jax.numpy as jnp
from jax import lax

PATCH = 16
NF = 8
BXP = 1
BYP = 4
BZP = 8
LEVELS = 3
BOTTOM = 16
OWNERS = 32
P_DEV = 32
PATCHES = 1024
CZ = 128
NX = 64
NY = 512
N_WIDE = 8
N_NARROW = 4


def slot_table(key):
    base = jax.random.fold_in(key, 11)
    subkeys = jax.random.split(base, 4)
    inward = jax.random.permutation(subkeys[0], OWNERS)
    outward = jax.random.permutation(subkeys[1], OWNERS)
    local_order = jax.vmap(lambda subkey: jax.random.permutation(subkey, P_DEV))(jax.random.split(subkeys[2], OWNERS))
    placing = jax.vmap(lambda subkey: jax.random.permutation(subkey, P_DEV))(jax.random.split(subkeys[3], OWNERS))
    offset = local_order // 2 % OWNERS
    destination = outward[(inward[:, None] + offset) % OWNERS]
    within = placing[destination, local_order]
    return (destination * P_DEV + within).reshape(-1).astype(jnp.int32)


def draw_target_slot(key, part):
    return slot_table(key)


def draw_fields(key, part):
    subkeys = jax.random.split(jax.random.fold_in(key, 23), 5)
    cells = PATCH ** 3
    velocity = jnp.clip(jax.random.normal(subkeys[1], (PATCHES, 3, cells), jnp.float32), -4.0, 4.0)
    density = jnp.exp(jax.random.uniform(subkeys[3], (PATCHES, 1, cells), jnp.float32, jnp.log(0.6), jnp.log(8.0)))
    carried = jnp.clip(jax.random.normal(subkeys[4], (PATCHES, NF - 4, cells), jnp.float32), -4.0, 4.0)
    return jnp.concatenate([velocity, density, carried], axis=1).astype(jnp.bfloat16)


def setup_inputs(seed: int = 0) -> dict:
    seeds = jax.random.split(jax.random.key(seed), 3)
    return {
        "target_slot": draw_target_slot(jax.random.fold_in(seeds[2], 71), 0),
        "fields": draw_fields(jax.random.fold_in(seeds[2], 71), 0),
    }


DAMPING = 0.8


def neighbours(values, direction):
    length = values.shape[direction]
    zero_plane = jnp.zeros_like(lax.slice_in_dim(values, 0, 1, axis=direction))
    lower_side = jnp.concatenate([zero_plane, lax.slice_in_dim(values, 0, length - 1, axis=direction)], direction)
    upper_side = jnp.concatenate([lax.slice_in_dim(values, 1, length, axis=direction), zero_plane], direction)
    return lower_side, upper_side


def face_along(density, direction):
    zero_plane = jnp.zeros_like(lax.slice_in_dim(density, 0, 1, axis=direction))
    padded = jnp.concatenate([zero_plane, density, zero_plane], direction)
    length = padded.shape[direction]
    return 2.0 / (lax.slice_in_dim(padded, 0, length - 1, axis=direction) + lax.slice_in_dim(padded, 1, length, axis=direction))


def split_faces(face, direction):
    length = face.shape[direction]
    return lax.slice_in_dim(face, 0, length - 1, axis=direction), lax.slice_in_dim(face, 1, length, axis=direction)


def apply_padded(values, face_set, level_scale):
    running = None
    for direction in range(3):
        lower_side, upper_side = neighbours(values, direction)
        low_face, high_face = split_faces(face_set[direction], direction)
        face_term = high_face * (values - upper_side) + low_face * (values - lower_side)
        running = face_term if running is None else running + face_term
    return level_scale * running


def diagonal_of(face_set, level_scale):
    running = None
    for direction in range(3):
        low_face, high_face = split_faces(face_set[direction], direction)
        face_term = low_face + high_face
        running = face_term if running is None else running + face_term
    return level_scale * running


def coarsen_faces(face_set):
    face_x, face_y, face_z = face_set
    picked = face_x[::2]
    coarse_x = picked.reshape(picked.shape[0], picked.shape[1] // 2, 2, picked.shape[2] // 2, 2).mean(axis=(2, 4))
    picked = face_y[:, ::2]
    coarse_y = picked.reshape(picked.shape[0] // 2, 2, picked.shape[1], picked.shape[2] // 2, 2).mean(axis=(1, 4))
    picked = face_z[:, :, ::2]
    coarse_z = picked.reshape(picked.shape[0] // 2, 2, picked.shape[1] // 2, 2, picked.shape[2]).mean(axis=(1, 3))
    return coarse_x, coarse_y, coarse_z


def restrict_mean(values):
    shape = values.shape
    return values.reshape(shape[0] // 2, 2, shape[1] // 2, 2, shape[2] // 2, 2).mean(axis=(1, 3, 5))


def prolong(values):
    return jnp.repeat(jnp.repeat(jnp.repeat(values, 2, axis=0), 2, axis=1), 2, axis=2)


def sweep_padded(values, source_term, face_set, diagonal, level_scale):
    return values + DAMPING * (source_term - apply_padded(values, face_set, level_scale)) / diagonal


def bottom_solve(source_term, face_set, level_scale):
    diagonal = diagonal_of(face_set, level_scale)

    def one_sweep(sweep_index, current):
        return sweep_padded(current, source_term, face_set, diagonal, level_scale)

    return lax.fori_loop(0, BOTTOM, one_sweep, jnp.zeros_like(source_term))


def project(grid_fields):
    velocity_x, velocity_y, velocity_z, density = grid_fields[0], grid_fields[1], grid_fields[2], grid_fields[3]
    face_set = tuple(face_along(density, direction) for direction in range(3))
    differences = []
    for direction, component in enumerate((velocity_x, velocity_y, velocity_z)):
        lower_side, upper_side = neighbours(component, direction)
        differences.append(upper_side - lower_side)
    source_term = -0.5 * ((differences[0] + differences[1]) + differences[2])
    stored = []
    for level_index in range(LEVELS):
        level_scale = 0.25 ** level_index
        diagonal = diagonal_of(face_set, level_scale)
        values = DAMPING * source_term / diagonal
        values = sweep_padded(values, source_term, face_set, diagonal, level_scale)
        residual = source_term - apply_padded(values, face_set, level_scale)
        stored.append((values, source_term, face_set, diagonal, level_scale))
        source_term = restrict_mean(residual)
        face_set = coarsen_faces(face_set)
    level_scale = 0.25 ** LEVELS
    slab_width = source_term.shape[1] // N_WIDE
    pieces = []
    for group_index in range(N_WIDE):
        start_row = group_index * slab_width
        slab_faces = (face_set[0][:, start_row:start_row + slab_width],
                      face_set[1][:, start_row:start_row + slab_width + 1],
                      face_set[2][:, start_row:start_row + slab_width])
        pieces.append(bottom_solve(source_term[:, start_row:start_row + slab_width], slab_faces, level_scale))
    correction = jnp.concatenate(pieces, 1)
    for level_index in reversed(range(LEVELS)):
        values, source_term, face_set, diagonal, level_scale = stored[level_index]
        values = values + prolong(correction)
        values = sweep_padded(values, source_term, face_set, diagonal, level_scale)
        values = sweep_padded(values, source_term, face_set, diagonal, level_scale)
        correction = values
    return correction


def reference(target_slot, fields):
    migrated = jnp.zeros_like(fields).at[target_slot].set(fields)
    solve_part = migrated[:, :4].reshape(N_WIDE, N_NARROW, BXP, BYP, BZP, 4, PATCH, PATCH, PATCH)
    grid_fields = jnp.transpose(solve_part, (5, 1, 2, 6, 0, 3, 7, 4, 8)).reshape(4, NX, NY, CZ).astype(jnp.float32)
    pressure = project(grid_fields)
    return migrated, pressure
```

```python
import functools

import jax
import jax.numpy as jnp
from jax import lax
from jax.experimental import pallas as pl
from jax.experimental.pallas import tpu as pltpu
from jax.sharding import PartitionSpec as P

PATCH = 16
BYP = 4
BZP = 8
LEVELS = 3
BOTTOM = 16
DAMPING = 0.8
KEEP = 1.0 - DAMPING
SOLVED = 4
CAPACITY = 2
X0 = PATCH
Y0 = PATCH * BYP
Z = PATCH * BZP
PAD = 8
MESH = pl.DeviceIdType.MESH
VMEM_LIMIT = 60 * 1024 * 1024


def dims(level):
    return X0 >> level, Y0 >> level


def pack_kernel(index_ref, fields_ref, solved_ref, carried_ref):
    def one(slot, carry):
        patch = fields_ref[index_ref[slot]]
        solved_ref[slot] = patch[:SOLVED]
        carried_ref[slot] = patch[SOLVED:]
        return carry

    lax.fori_loop(0, solved_ref.shape[0], one, 0)


def merge_kernel(index_ref, solved_ref, carried_ref, out_ref):
    def one(patch, carry):
        row = index_ref[patch]
        out_ref[patch, :SOLVED] = solved_ref[row]
        out_ref[patch, SOLVED:] = carried_ref[row]
        return carry

    lax.fori_loop(0, out_ref.shape[0], one, 0)


def solve_kernel(
    n_wide,
    n_narrow,
    index_ref,
    arrived_ref,
    out_ref,
    turn,
    tmp,
    grid_u,
    grid_v,
    grid_w,
    grid_r,
    field_sent,
    field_got,
    iterates,
    sent_rows,
    got_rows,
    face_x,
    face_yl,
    face_yh,
    face_zl,
    face_zh,
    diag,
    weight,
    source,
    answer,
    gather_faces,
    gather_source,
    coef,
    send_sem,
    recv_sem,
    gsend_sem,
    grecv_sem,
):
    wide = lax.axis_index("wide")
    narrow = lax.axis_index("narrow")
    has = {
        "xl": narrow > 0,
        "xh": narrow < n_narrow - 1,
        "yl": wide > 0,
        "yh": wide < n_wide - 1,
    }
    peer = {
        "xl": (wide, narrow - 1),
        "xh": (wide, narrow + 1),
        "yl": (wide - 1, narrow),
        "yh": (wide + 1, narrow),
    }
    order = ("xl", "xh", "yl", "yh")
    others = [(wide, lax.rem(narrow + d, n_narrow)) for d in range(1, n_narrow)]

    barrier = pltpu.get_barrier_semaphore()
    beside = [(lax.rem(wide + d, n_wide), narrow) for d in (1, n_wide - 1)]
    for other in others + beside:
        pl.semaphore_signal(barrier, inc=1, device_id=other, device_id_type=MESH)
    pl.semaphore_wait(barrier, len(others) + len(beside))

    lane = lax.broadcasted_iota(jnp.int32, (8, Z), 1)
    block_lane = lane // PATCH

    lower_bits = [(block_lane // s) % 2 == 1 for s in (1, 2, 4)]

    def to_grid(step, carry):
        b = step // X0
        i = step % X0
        at = pl.multiple_of(i * 2 * Z, 2 * Z)
        rows = []
        for c in range(BZP):
            both = arrived_ref[index_ref[b * BZP + c], :, pl.ds(at, 2 * Z)].astype(
                jnp.float32
            )
            rows.append(jnp.concatenate([both[:, :Z], both[:, Z:]], axis=0))
        for bit, s in zip(lower_bits, (1, 2, 4)):
            new = list(rows)
            for c in range(BZP):
                if c & s == 0:
                    low, high = rows[c], rows[c + s]
                    new[c] = jnp.where(bit, pltpu.roll(high, PATCH * s, 1), low)
                    new[c + s] = jnp.where(bit, high, pltpu.roll(low, Z - PATCH * s, 1))
            rows = new
        for j in range(8):
            turn[8 * j : 8 * j + 8, :] = rows[j]
        for half in range(2):
            y = pl.multiple_of(b * PATCH + half * 8, 8)
            for f, ref in enumerate((grid_u, grid_v, grid_w, grid_r)):
                values = turn[pl.ds(half * SOLVED + f, 8, stride=8), :]
                if f == 2:
                    ref[i, pl.ds(y, 8), :] = values
                else:
                    ref[i + 1, pl.ds(PAD + y, 8), :] = values
        return carry

    lax.fori_loop(0, BYP * X0, to_grid, 0)

    def exchange(padded, X, Y, sent, got, slot, sides):
        mid = pl.ds(PAD, Y)
        ends = {
            "xl": (lambda: padded.at[1, mid], lambda: padded.at[X + 1, mid]),
            "xh": (lambda: padded.at[X, mid], lambda: padded.at[0, mid]),
            "yl": (lambda: sent.at[0], lambda: got.at[1]),
            "yh": (lambda: sent.at[1], lambda: got.at[0]),
        }
        back = {"xl": "xh", "xh": "xl", "yl": "yh", "yh": "yl"}

        def copy(side):
            src, dst = ends[side]
            return pltpu.make_async_remote_copy(
                src_ref=src(),
                dst_ref=dst(),
                send_sem=send_sem.at[slot, order.index(side)],
                recv_sem=recv_sem.at[slot, order.index(back[side])],
                device_id=peer[side],
                device_id_type=MESH,
            )

        def landing(side):
            src, dst = ends[back[side]]
            return pltpu.make_async_remote_copy(
                src_ref=src(),
                dst_ref=dst(),
                send_sem=send_sem.at[slot, order.index(side)],
                recv_sem=recv_sem.at[slot, order.index(side)],
                device_id=peer[side],
                device_id_type=MESH,
            )

        def start():
            for side in sides:

                @pl.when(has[side])
                def _():
                    copy(side).start()

        def finish():
            for side in sides:

                @pl.when(has[side])
                def _():
                    landing(side).wait_recv()

                @pl.when(jnp.logical_not(has[side]))
                def _():
                    if side == "xl":
                        padded[0, PAD : PAD + Y, :] = jnp.zeros((Y, Z), jnp.float32)
                    elif side == "xh":
                        padded[X + 1, PAD : PAD + Y, :] = jnp.zeros((Y, Z), jnp.float32)
                    elif side == "yl":
                        got[0] = jnp.zeros((X, Z), jnp.float32)
                    else:
                        got[1] = jnp.zeros((X, Z), jnp.float32)

            if "yl" in sides:

                for x in range(X):
                    padded[x + 1, PAD - 1 : PAD, :] = got[0, x : x + 1, :]
                    padded[x + 1, PAD + Y : PAD + Y + 1, :] = got[1, x : x + 1, :]

        def drain():
            for side in sides:

                @pl.when(has[side])
                def _():
                    copy(side).wait_send()

        return start, finish, drain

    drains = []

    for k, ref in ((0, grid_v), (1, grid_r)):
        for x in range(X0):
            field_sent[k, 0, x : x + 1, :] = ref[x + 1, PAD : PAD + 1, :]
            field_sent[k, 1, x : x + 1, :] = ref[x + 1, PAD + Y0 - 1 : PAD + Y0, :]
    field_moves = [
        exchange(grid_r, X0, Y0, field_sent.at[1], field_got.at[1], 0, order),
        exchange(grid_u, X0, Y0, None, None, 1, ("xl", "xh")),
        exchange(grid_v, X0, Y0, field_sent.at[0], field_got.at[0], 2, ("yl", "yh")),
    ]
    for start, finish, drain in field_moves:
        start()
        drains.append(drain)
    for start, finish, drain in field_moves:
        finish()

    def z_low(values, step):
        rolled = pltpu.roll(values, step, 1)
        at = lax.broadcasted_iota(jnp.int32, values.shape, 1)
        return jnp.where(at < step, 0.0, rolled)

    def z_high(values, step):
        rolled = pltpu.roll(values, Z - step, 1)
        at = lax.broadcasted_iota(jnp.int32, values.shape, 1)
        return jnp.where(at >= Z - step, 0.0, rolled)

    mid0 = pl.ds(PAD, Y0)

    def first(x, carry):
        here = grid_r[x + 1, mid0, :]
        fxl = 2.0 / (grid_r[x, mid0, :] + here)
        fxh = 2.0 / (here + grid_r[x + 2, mid0, :])
        fyl = 2.0 / (grid_r[x + 1, PAD - 1 : PAD - 1 + Y0, :] + here)
        fyh = 2.0 / (grid_r[x + 1, PAD + 1 : PAD + 1 + Y0, :] + here)
        fzl = 2.0 / (z_low(here, 1) + here)
        fzh = 2.0 / (z_high(here, 1) + here)
        face_x[0][x] = fxl
        face_x[0][x + 1] = fxh
        face_yl[0][x] = fyl
        face_yh[0][x] = fyh
        face_zl[0][x] = fzl
        face_zh[0][x] = fzh
        total = ((fxl + fxh) + (fyl + fyh)) + (fzl + fzh)
        diag[0][x] = total
        weight[0][x] = DAMPING / total
        w = grid_w[x]
        du = grid_u[x + 2, mid0, :] - grid_u[x, mid0, :]
        dv = (
            grid_v[x + 1, PAD + 1 : PAD + 1 + Y0, :]
            - grid_v[x + 1, PAD - 1 : PAD - 1 + Y0, :]
        )
        source[0][x] = -0.5 * ((du + dv) + (z_high(w, 1) - z_low(w, 1)))
        return carry

    lax.fori_loop(0, X0, first, 0)

    def z_bit(shape, level):
        at = lax.broadcasted_iota(jnp.int32, shape, 1)
        return (at // (1 << level)) % 2 == 1

    def z_pair(values, level):
        step = 1 << level
        other = jnp.where(
            z_bit(values.shape, level),
            pltpu.roll(values, step, 1),
            pltpu.roll(values, Z - step, 1),
        )
        return values + other

    def z_even(values, level):
        step = 1 << level
        return jnp.where(
            z_bit(values.shape, level), pltpu.roll(values, step, 1), values
        )

    def z_odd(values, level):
        step = 1 << level
        return jnp.where(
            z_bit(values.shape, level), values, pltpu.roll(values, Z - step, 1)
        )

    for level in range(LEVELS):
        X, Y = dims(level + 1)
        even, odd = pl.ds(0, Y, stride=2), pl.ds(1, Y, stride=2)
        last = level + 1 == LEVELS

        def coarse_x(x, level=level, even=even, odd=odd):
            fx = face_x[level]
            return 0.25 * z_pair(fx[2 * x, even, :] + fx[2 * x, odd, :], level)

        def coarse_rest(x, level=level, even=even, odd=odd):
            yl, yh = face_yl[level], face_yh[level]
            zl, zh = face_zl[level], face_zh[level]
            fyl = 0.25 * z_pair(yl[2 * x, even, :] + yl[2 * x + 1, even, :], level)
            fyh = 0.25 * z_pair(yh[2 * x, odd, :] + yh[2 * x + 1, odd, :], level)
            four_l = (zl[2 * x, even, :] + zl[2 * x, odd, :]) + (
                zl[2 * x + 1, even, :] + zl[2 * x + 1, odd, :]
            )
            four_h = (zh[2 * x, even, :] + zh[2 * x, odd, :]) + (
                zh[2 * x + 1, even, :] + zh[2 * x + 1, odd, :]
            )
            return fyl, fyh, z_even(0.25 * four_l, level), z_odd(0.25 * four_h, level)

        if last:
            for x in range(X + 1):
                gather_faces[narrow, x] = coarse_x(x)
            for x in range(X):
                for k, face in enumerate(coarse_rest(x)):
                    gather_faces[narrow, X + 1 + k * X + x] = face
        else:

            def planes(x, carry, level=level, rest=coarse_rest, cx=coarse_x):
                fxl, fxh = cx(x), cx(x + 1)
                fyl, fyh, fzl, fzh = rest(x)
                face_x[level + 1][x] = fxl
                face_x[level + 1][x + 1] = fxh
                face_yl[level + 1][x] = fyl
                face_yh[level + 1][x] = fyh
                face_zl[level + 1][x] = fzl
                face_zh[level + 1][x] = fzh
                total = ((fxl + fxh) + (fyl + fyh)) + (fzl + fzh)
                diag[level + 1][x] = total
                weight[level + 1][x] = DAMPING / total
                return carry

            lax.fori_loop(0, X, planes, 0)

    def gather(ref, which):
        def copy(d):
            return pltpu.make_async_remote_copy(
                src_ref=ref.at[narrow],
                dst_ref=ref.at[narrow],
                send_sem=gsend_sem.at[which, d - 1],
                recv_sem=grecv_sem.at[which, d - 1],
                device_id=others[d - 1],
                device_id_type=MESH,
            )

        def landing(d):
            came = lax.rem(narrow + n_narrow - d, n_narrow)
            return pltpu.make_async_remote_copy(
                src_ref=ref.at[narrow],
                dst_ref=ref.at[came],
                send_sem=gsend_sem.at[which, d - 1],
                recv_sem=grecv_sem.at[which, d - 1],
                device_id=others[d - 1],
                device_id_type=MESH,
            )

        def start():
            for d in range(1, n_narrow):
                copy(d).start()

        def finish():
            for d in range(1, n_narrow):
                landing(d).wait_recv()

        def drain():
            for d in range(1, n_narrow):
                copy(d).wait_send()

        return start, finish, drain

    face_start, face_finish, face_drain = gather(gather_faces, 0)
    source_start, source_finish, source_drain = gather(gather_source, 1)
    face_start()

    def neighbour_sum(level, e, x):
        _, Y = dims(level)
        p = iterates[level]
        step = 1 << level
        mid = pl.ds(PAD, Y)
        here = p[e, x + 1, mid, :]
        total = (
            face_x[level][x] * p[e, x, mid, :]
            + face_x[level][x + 1] * p[e, x + 2, mid, :]
        )
        total += face_yl[level][x] * p[e, x + 1, PAD - 1 : PAD - 1 + Y, :]
        total += face_yh[level][x] * p[e, x + 1, PAD + 1 : PAD + 1 + Y, :]
        total += face_zl[level][x] * z_low(here, step)
        total += face_zh[level][x] * z_high(here, step)
        return here, total

    def sweep(level, e, x):
        here, total = neighbour_sum(level, e, x)
        return KEEP * here + weight[level][x] * (source[level][x] + total)

    def produce(level, e, values_of):
        X, Y = dims(level)
        p = iterates[level]

        def plane(x, carry):
            v = values_of(x)
            p[e, x + 1, PAD : PAD + Y, :] = v
            sent_rows[level][e, 0, pl.ds(x, 1), :] = v[:1]
            sent_rows[level][e, 1, pl.ds(x, 1), :] = v[Y - 1 :]
            return carry

        lax.fori_loop(0, X, plane, 0)
        start, finish, drain = exchange(
            p.at[e],
            X,
            Y,
            sent_rows[level].at[e],
            got_rows[level].at[e],
            3 + 4 * level + e,
            order,
        )
        start()
        drains.append(drain)
        finish()

    for level in range(LEVELS):
        X, Y = dims(level)
        produce(level, 0, lambda x, level=level: weight[level][x] * source[level][x])
        produce(level, 1, lambda x, level=level: sweep(level, 0, x))

        def restrict(x, carry, level=level, Y=Y):
            both = None
            for k in range(2):
                here, total = neighbour_sum(level, 1, 2 * x + k)
                left = (source[level][2 * x + k] - diag[level][2 * x + k] * here) + total
                both = left if both is None else both + left
            tmp[:Y, :] = both
            half = Y // 2
            summed = (
                tmp[pl.ds(0, half, stride=2), :] + tmp[pl.ds(1, half, stride=2), :]
            )
            summed = 0.5 * z_pair(summed, level)
            if level + 1 == LEVELS:
                gather_source[narrow, x] = summed
            else:
                source[level + 1][x] = summed
            return carry

        if level + 1 == LEVELS:
            for x in range(X // 2):
                restrict(x, 0)
        else:
            lax.fori_loop(0, X // 2, restrict, 0)

    source_start()
    face_finish()
    source_finish()
    X, Y = dims(LEVELS)
    step = 1 << LEVELS
    row = lax.broadcasted_iota(jnp.int32, (Y, Z), 0)
    col = lax.broadcasted_iota(jnp.int32, (Y, Z), 1)
    for n in range(n_narrow):
        for x in range(X):
            fxl, fxh = gather_faces[n, x], gather_faces[n, x + 1]
            fyl, fyh, fzl, fzh = (gather_faces[n, X + 1 + k * X + x] for k in range(4))
            total = ((fxl + fxh) + (fyl + fyh)) + (fzl + fzh)
            w = DAMPING / total
            at = n * X + x
            coef[0, at] = w * fxl
            coef[1, at] = w * fxh
            coef[2, at] = jnp.where(row == 0, 0.0, w * fyl)
            coef[3, at] = jnp.where(row == Y - 1, 0.0, w * fyh)
            coef[4, at] = jnp.where(col < step, 0.0, w * fzl)
            coef[5, at] = jnp.where(col >= Z - step, 0.0, w * fzh)
            coef[6, at] = w * gather_source[n, x]

    zero_plane = jnp.zeros((1, Y, Z), jnp.float32)

    def bottom(k, cur):
        new = KEEP * cur + coef[6]
        new += coef[0] * jnp.concatenate([zero_plane, cur[:-1]], axis=0)
        new += coef[1] * jnp.concatenate([cur[1:], zero_plane], axis=0)
        new += coef[2] * pltpu.roll(cur, 1, 1)
        new += coef[3] * pltpu.roll(cur, Y - 1, 1)
        new += coef[4] * pltpu.roll(cur, step, 2)
        new += coef[5] * pltpu.roll(cur, Z - step, 2)
        return new

    coef[7] = lax.fori_loop(0, BOTTOM - 1, bottom, coef[6])
    for x in range(X):
        answer[LEVELS][x] = coef[7, narrow * X + x]

    for level in reversed(range(LEVELS)):
        X, Y = dims(level)
        half = Y // 2

        def raised(x, level=level, Y=Y, half=half):
            e = answer[level + 1][x // 2]
            tmp[pl.ds(0, half, stride=2), :] = e
            tmp[pl.ds(1, half, stride=2), :] = e
            return iterates[level][1, x + 1, PAD : PAD + Y, :] + tmp[:Y, :]

        produce(level, 2, raised)
        produce(level, 3, lambda x, level=level: sweep(level, 2, x))
        target = out_ref if level == 0 else answer[level]

        def close(x, carry, level=level, target=target):
            target[x] = sweep(level, 3, x)
            return carry

        lax.fori_loop(0, X, close, 0)

    face_drain()
    source_drain()
    for drain in drains:
        drain()


def f32(*shape):
    return pltpu.VMEM(shape, jnp.float32)


def call_solve(n_wide, n_narrow, receive_index, arrived):
    X3, Y3 = dims(LEVELS)
    levels = [dims(level) for level in range(LEVELS)]
    padded = f32(X0 + 2, Y0 + 2 * PAD, Z)
    each = [f32(X, Y, Z) for X, Y in levels]
    moves = 3 + 4 * LEVELS
    scratch = [
        f32(64, Z),
        f32(Y0, Z),
        padded,
        padded,
        f32(X0, Y0, Z),
        padded,
        f32(2, 2, X0, Z),
        f32(2, 2, X0, Z),
        [f32(4, X + 2, Y + 2 * PAD, Z) for X, Y in levels],
        [f32(4, 2, X, Z) for X, Y in levels],
        [f32(4, 2, X, Z) for X, Y in levels],
        [f32(X + 1, Y, Z) for X, Y in levels],
        each,
        each,
        each,
        each,
        each,
        each,
        each,
        [f32(*dims(level), Z) for level in range(LEVELS + 1)],
        f32(n_narrow, 5 * X3 + 1, Y3, Z),
        f32(n_narrow, X3, Y3, Z),
        f32(8, n_narrow * X3, Y3, Z),
        pltpu.SemaphoreType.DMA((moves, 4)),
        pltpu.SemaphoreType.DMA((moves, 4)),
        pltpu.SemaphoreType.DMA((2, n_narrow - 1)),
        pltpu.SemaphoreType.DMA((2, n_narrow - 1)),
    ]
    return pl.pallas_call(
        functools.partial(solve_kernel, n_wide, n_narrow),
        out_shape=jax.ShapeDtypeStruct((X0, Y0, Z), jnp.float32),
        in_specs=[
            pl.BlockSpec(memory_space=pltpu.SMEM),
            pl.BlockSpec(memory_space=pltpu.VMEM),
        ],
        out_specs=pl.BlockSpec(memory_space=pltpu.VMEM),
        scratch_shapes=scratch,
        compiler_params=pltpu.CompilerParams(
            collective_id=0, has_side_effects=True, vmem_limit_bytes=VMEM_LIMIT
        ),
        cost_estimate=pl.CostEstimate(
            flops=200_000_000, bytes_accessed=200_000_000, transcendentals=0
        ),
    )(receive_index, arrived)


def shards(n_wide, n_narrow, target_slot, fields):
    per_owner, n_fields, cells = fields.shape
    owners = n_wide * n_narrow
    me = lax.axis_index("wide") * n_narrow + lax.axis_index("narrow")
    slots = owners * CAPACITY
    place = jnp.arange(per_owner, dtype=jnp.int32)
    own_target = lax.dynamic_slice_in_dim(target_slot, me * per_owner, per_owner) // per_owner
    earlier = jnp.sum(
        (
            (own_target[:, None] == own_target[None, :]) & (place[:, None] > place[None, :])
        ).astype(jnp.int32),
        axis=1,
    )
    own_slot = own_target * CAPACITY + earlier
    slot_ids = jnp.arange(slots, dtype=jnp.int32)
    send_index = jnp.sum(
        jnp.where(own_slot[None, :] == slot_ids[:, None], place[None, :], 0), axis=1
    )
    table = target_slot.reshape(owners, per_owner)
    to_me = table // per_owner == me
    rank = jnp.sum(
        (to_me[:, None, :] & (place[None, :, None] > place[None, None, :])).astype(jnp.int32),
        axis=2,
    )
    row = jnp.arange(owners, dtype=jnp.int32)[:, None] * CAPACITY + rank
    receive_index = jnp.sum(
        jnp.where(
            target_slot[None, :] == (me * per_owner + place)[:, None], row.reshape(-1)[None, :], 0
        ),
        axis=1,
    )

    smem = pl.BlockSpec(memory_space=pltpu.SMEM)
    vmem = pl.BlockSpec(memory_space=pltpu.VMEM)
    params = pltpu.CompilerParams(vmem_limit_bytes=VMEM_LIMIT)
    carried_fields = n_fields - SOLVED
    solved, carried = pl.pallas_call(
        pack_kernel,
        out_shape=(
            jax.ShapeDtypeStruct((slots, SOLVED, cells), fields.dtype),
            jax.ShapeDtypeStruct((slots, carried_fields, cells), fields.dtype),
        ),
        in_specs=[smem, vmem],
        out_specs=(vmem, vmem),
        compiler_params=params,
    )(send_index, fields)
    swap = functools.partial(
        lax.all_to_all,
        axis_name=("wide", "narrow"),
        split_axis=0,
        concat_axis=0,
        tiled=True,
    )
    solved = swap(solved)
    solved, carried = lax.optimization_barrier((solved, carried))
    carried = swap(carried)
    pressure = call_solve(n_wide, n_narrow, receive_index, solved)
    migrated = pl.pallas_call(
        merge_kernel,
        out_shape=jax.ShapeDtypeStruct(fields.shape, fields.dtype),
        in_specs=[smem, vmem, vmem],
        out_specs=vmem,
        compiler_params=params,
    )(receive_index, solved, carried)
    return migrated, pressure


def solution(mesh):
    body = functools.partial(shards, mesh.shape["wide"], mesh.shape["narrow"])
    in_specs = (P(), P(("wide", "narrow"), None, None))
    out_specs = (P(("wide", "narrow"), None, None), P("narrow", "wide", None))
    return jax.shard_map(body, mesh=mesh, in_specs=in_specs, out_specs=out_specs, check_vma=False)
```

```python
import functools

import jax
import jax.numpy as jnp
from jax import lax
from jax.experimental import pallas as pl
from jax.experimental.pallas import tpu as pltpu
from jax.sharding import PartitionSpec as P

PATCH = 16
BYP = 4
BZP = 8
LEVELS = 3
BOTTOM = 16
DAMPING = 0.8
KEEP = 1.0 - DAMPING
SOLVED = 4
CAPACITY = 2
X0 = PATCH
Y0 = PATCH * BYP
Z = PATCH * BZP
PAD = 8
MESH = pl.DeviceIdType.MESH
VMEM_LIMIT = 60 * 1024 * 1024


def dims(level):
    return X0 >> level, Y0 >> level


def pack_kernel(index_ref, fields_ref, solved_ref, carried_ref):
    def one(slot, carry):
        patch = fields_ref[index_ref[slot]]
        solved_ref[slot] = patch[:SOLVED]
        carried_ref[slot] = patch[SOLVED:]
        return carry

    lax.fori_loop(0, solved_ref.shape[0], one, 0, unroll=4)


def merge_kernel(index_ref, solved_ref, carried_ref, out_ref):
    def one(patch, carry):
        row = index_ref[patch]
        out_ref[patch, :SOLVED] = solved_ref[row]
        out_ref[patch, SOLVED:] = carried_ref[row]
        return carry

    lax.fori_loop(0, out_ref.shape[0], one, 0, unroll=4)


def solve_kernel(
    n_wide,
    n_narrow,
    index_ref,
    arrived_ref,
    out_ref,
    turn,
    tmp,
    grid_u,
    grid_v,
    grid_w,
    grid_r,
    field_sent,
    field_got,
    iterates,
    sent_rows,
    got_rows,
    face_x,
    face_yl,
    face_yh,
    face_zl,
    face_zh,
    diag,
    weight,
    source,
    answer,
    gather_faces,
    gather_source,
    coef,
    send_sem,
    recv_sem,
    gsend_sem,
    grecv_sem,
):
    wide = lax.axis_index("wide")
    narrow = lax.axis_index("narrow")
    has = {
        "xl": narrow > 0,
        "xh": narrow < n_narrow - 1,
        "yl": wide > 0,
        "yh": wide < n_wide - 1,
    }
    peer = {
        "xl": (wide, narrow - 1),
        "xh": (wide, narrow + 1),
        "yl": (wide - 1, narrow),
        "yh": (wide + 1, narrow),
    }
    order = ("xl", "xh", "yl", "yh")
    others = [(wide, lax.rem(narrow + d, n_narrow)) for d in range(1, n_narrow)]

    barrier = pltpu.get_barrier_semaphore()
    beside = [(lax.rem(wide + d, n_wide), narrow) for d in (1, n_wide - 1)]
    for other in others + beside:
        pl.semaphore_signal(barrier, inc=1, device_id=other, device_id_type=MESH)
    pl.semaphore_wait(barrier, len(others) + len(beside))

    lane = lax.broadcasted_iota(jnp.int32, (8, Z), 1)
    block_lane = lane // PATCH

    lower_bits = [(block_lane // s) % 2 == 1 for s in (1, 2, 4)]

    def to_grid(step, carry):
        b = step // X0
        i = step % X0
        at = pl.multiple_of(i * 2 * Z, 2 * Z)
        rows = []
        for c in range(BZP):
            both = arrived_ref[index_ref[b * BZP + c], :, pl.ds(at, 2 * Z)].astype(
                jnp.float32
            )
            rows.append(jnp.concatenate([both[:, :Z], both[:, Z:]], axis=0))
        for bit, s in zip(lower_bits, (1, 2, 4)):
            new = list(rows)
            for c in range(BZP):
                if c & s == 0:
                    low, high = rows[c], rows[c + s]
                    new[c] = jnp.where(bit, pltpu.roll(high, PATCH * s, 1), low)
                    new[c + s] = jnp.where(bit, high, pltpu.roll(low, Z - PATCH * s, 1))
            rows = new
        for j in range(8):
            turn[8 * j : 8 * j + 8, :] = rows[j]
        for half in range(2):
            y = pl.multiple_of(b * PATCH + half * 8, 8)
            for f, ref in enumerate((grid_u, grid_v, grid_w, grid_r)):
                values = turn[pl.ds(half * SOLVED + f, 8, stride=8), :]
                if f == 2:
                    ref[i, pl.ds(y, 8), :] = values
                else:
                    ref[i + 1, pl.ds(PAD + y, 8), :] = values
        return carry

    lax.fori_loop(0, BYP * X0, to_grid, 0, unroll=4)

    def exchange(padded, X, Y, sent, got, slot, sides):
        mid = pl.ds(PAD, Y)
        ends = {
            "xl": (lambda: padded.at[1, mid], lambda: padded.at[X + 1, mid]),
            "xh": (lambda: padded.at[X, mid], lambda: padded.at[0, mid]),
            "yl": (lambda: sent.at[0], lambda: got.at[1]),
            "yh": (lambda: sent.at[1], lambda: got.at[0]),
        }
        back = {"xl": "xh", "xh": "xl", "yl": "yh", "yh": "yl"}

        def copy(side):
            src, dst = ends[side]
            return pltpu.make_async_remote_copy(
                src_ref=src(),
                dst_ref=dst(),
                send_sem=send_sem.at[slot, order.index(side)],
                recv_sem=recv_sem.at[slot, order.index(back[side])],
                device_id=peer[side],
                device_id_type=MESH,
            )

        def landing(side):
            src, dst = ends[back[side]]
            return pltpu.make_async_remote_copy(
                src_ref=src(),
                dst_ref=dst(),
                send_sem=send_sem.at[slot, order.index(side)],
                recv_sem=recv_sem.at[slot, order.index(side)],
                device_id=peer[side],
                device_id_type=MESH,
            )

        def start():
            for side in sides:

                @pl.when(has[side])
                def _():
                    copy(side).start()

        def finish():
            for side in sides:

                @pl.when(has[side])
                def _():
                    landing(side).wait_recv()

                @pl.when(jnp.logical_not(has[side]))
                def _():
                    if side == "xl":
                        padded[0, PAD : PAD + Y, :] = jnp.zeros((Y, Z), jnp.float32)
                    elif side == "xh":
                        padded[X + 1, PAD : PAD + Y, :] = jnp.zeros((Y, Z), jnp.float32)
                    elif side == "yl":
                        got[0] = jnp.zeros((X, Z), jnp.float32)
                    else:
                        got[1] = jnp.zeros((X, Z), jnp.float32)

            if "yl" in sides:

                for x in range(X):
                    padded[x + 1, PAD - 1 : PAD, :] = got[0, x : x + 1, :]
                    padded[x + 1, PAD + Y : PAD + Y + 1, :] = got[1, x : x + 1, :]

        def drain():
            for side in sides:

                @pl.when(has[side])
                def _():
                    copy(side).wait_send()

        return start, finish, drain

    drains = []

    for k, ref in ((0, grid_v), (1, grid_r)):
        for x in range(X0):
            field_sent[k, 0, x : x + 1, :] = ref[x + 1, PAD : PAD + 1, :]
            field_sent[k, 1, x : x + 1, :] = ref[x + 1, PAD + Y0 - 1 : PAD + Y0, :]
    field_moves = [
        exchange(grid_r, X0, Y0, field_sent.at[1], field_got.at[1], 0, order),
        exchange(grid_u, X0, Y0, None, None, 1, ("xl", "xh")),
        exchange(grid_v, X0, Y0, field_sent.at[0], field_got.at[0], 2, ("yl", "yh")),
    ]
    for start, finish, drain in field_moves:
        start()
        drains.append(drain)
    for start, finish, drain in field_moves:
        finish()

    def z_low(values, step):
        rolled = pltpu.roll(values, step, 1)
        at = lax.broadcasted_iota(jnp.int32, values.shape, 1)
        return jnp.where(at < step, 0.0, rolled)

    def z_high(values, step):
        rolled = pltpu.roll(values, Z - step, 1)
        at = lax.broadcasted_iota(jnp.int32, values.shape, 1)
        return jnp.where(at >= Z - step, 0.0, rolled)

    mid0 = pl.ds(PAD, Y0)

    def first(x, carry):
        here = grid_r[x + 1, mid0, :]
        fxl = 2.0 / (grid_r[x, mid0, :] + here)
        fxh = 2.0 / (here + grid_r[x + 2, mid0, :])
        fyl = 2.0 / (grid_r[x + 1, PAD - 1 : PAD - 1 + Y0, :] + here)
        fyh = 2.0 / (grid_r[x + 1, PAD + 1 : PAD + 1 + Y0, :] + here)
        fzl = 2.0 / (z_low(here, 1) + here)
        fzh = 2.0 / (z_high(here, 1) + here)
        face_x[0][x] = fxl
        face_x[0][x + 1] = fxh
        face_yl[0][x] = fyl
        face_yh[0][x] = fyh
        face_zl[0][x] = fzl
        face_zh[0][x] = fzh
        total = ((fxl + fxh) + (fyl + fyh)) + (fzl + fzh)
        diag[0][x] = total
        weight[0][x] = DAMPING / total
        w = grid_w[x]
        du = grid_u[x + 2, mid0, :] - grid_u[x, mid0, :]
        dv = (
            grid_v[x + 1, PAD + 1 : PAD + 1 + Y0, :]
            - grid_v[x + 1, PAD - 1 : PAD - 1 + Y0, :]
        )
        source[0][x] = -0.5 * ((du + dv) + (z_high(w, 1) - z_low(w, 1)))
        return carry

    lax.fori_loop(0, X0, first, 0, unroll=4)

    def z_bit(shape, level):
        at = lax.broadcasted_iota(jnp.int32, shape, 1)
        return (at // (1 << level)) % 2 == 1

    def z_pair(values, level):
        step = 1 << level
        other = jnp.where(
            z_bit(values.shape, level),
            pltpu.roll(values, step, 1),
            pltpu.roll(values, Z - step, 1),
        )
        return values + other

    def z_even(values, level):
        step = 1 << level
        return jnp.where(
            z_bit(values.shape, level), pltpu.roll(values, step, 1), values
        )

    def z_odd(values, level):
        step = 1 << level
        return jnp.where(
            z_bit(values.shape, level), values, pltpu.roll(values, Z - step, 1)
        )

    for level in range(LEVELS):
        X, Y = dims(level + 1)
        even, odd = pl.ds(0, Y, stride=2), pl.ds(1, Y, stride=2)
        last = level + 1 == LEVELS

        def coarse_x(x, level=level, even=even, odd=odd):
            fx = face_x[level]
            return 0.25 * z_pair(fx[2 * x, even, :] + fx[2 * x, odd, :], level)

        def coarse_rest(x, level=level, even=even, odd=odd):
            yl, yh = face_yl[level], face_yh[level]
            zl, zh = face_zl[level], face_zh[level]
            fyl = 0.25 * z_pair(yl[2 * x, even, :] + yl[2 * x + 1, even, :], level)
            fyh = 0.25 * z_pair(yh[2 * x, odd, :] + yh[2 * x + 1, odd, :], level)
            four_l = (zl[2 * x, even, :] + zl[2 * x, odd, :]) + (
                zl[2 * x + 1, even, :] + zl[2 * x + 1, odd, :]
            )
            four_h = (zh[2 * x, even, :] + zh[2 * x, odd, :]) + (
                zh[2 * x + 1, even, :] + zh[2 * x + 1, odd, :]
            )
            return fyl, fyh, z_even(0.25 * four_l, level), z_odd(0.25 * four_h, level)

        if last:
            for x in range(X + 1):
                gather_faces[narrow, x] = coarse_x(x)
            for x in range(X):
                for k, face in enumerate(coarse_rest(x)):
                    gather_faces[narrow, X + 1 + k * X + x] = face
        else:

            def planes(x, carry, level=level, rest=coarse_rest, cx=coarse_x):
                fxl, fxh = cx(x), cx(x + 1)
                fyl, fyh, fzl, fzh = rest(x)
                face_x[level + 1][x] = fxl
                face_x[level + 1][x + 1] = fxh
                face_yl[level + 1][x] = fyl
                face_yh[level + 1][x] = fyh
                face_zl[level + 1][x] = fzl
                face_zh[level + 1][x] = fzh
                total = ((fxl + fxh) + (fyl + fyh)) + (fzl + fzh)
                diag[level + 1][x] = total
                weight[level + 1][x] = DAMPING / total
                return carry

            lax.fori_loop(0, X, planes, 0, unroll=4)

    def gather(ref, which):
        def copy(d):
            return pltpu.make_async_remote_copy(
                src_ref=ref.at[narrow],
                dst_ref=ref.at[narrow],
                send_sem=gsend_sem.at[which, d - 1],
                recv_sem=grecv_sem.at[which, d - 1],
                device_id=others[d - 1],
                device_id_type=MESH,
            )

        def landing(d):
            came = lax.rem(narrow + n_narrow - d, n_narrow)
            return pltpu.make_async_remote_copy(
                src_ref=ref.at[narrow],
                dst_ref=ref.at[came],
                send_sem=gsend_sem.at[which, d - 1],
                recv_sem=grecv_sem.at[which, d - 1],
                device_id=others[d - 1],
                device_id_type=MESH,
            )

        def start():
            for d in range(1, n_narrow):
                copy(d).start()

        def finish():
            for d in range(1, n_narrow):
                landing(d).wait_recv()

        def drain():
            for d in range(1, n_narrow):
                copy(d).wait_send()

        return start, finish, drain

    face_start, face_finish, face_drain = gather(gather_faces, 0)
    source_start, source_finish, source_drain = gather(gather_source, 1)
    face_start()

    def neighbour_sum(level, e, x):
        _, Y = dims(level)
        p = iterates[level]
        step = 1 << level
        mid = pl.ds(PAD, Y)
        here = p[e, x + 1, mid, :]
        total = (
            face_x[level][x] * p[e, x, mid, :]
            + face_x[level][x + 1] * p[e, x + 2, mid, :]
        )
        total += face_yl[level][x] * p[e, x + 1, PAD - 1 : PAD - 1 + Y, :]
        total += face_yh[level][x] * p[e, x + 1, PAD + 1 : PAD + 1 + Y, :]
        total += face_zl[level][x] * z_low(here, step)
        total += face_zh[level][x] * z_high(here, step)
        return here, total

    def sweep(level, e, x):
        here, total = neighbour_sum(level, e, x)
        return KEEP * here + weight[level][x] * (source[level][x] + total)

    def produce(level, e, values_of):
        X, Y = dims(level)
        p = iterates[level]

        def plane(x, carry):
            v = values_of(x)
            p[e, x + 1, PAD : PAD + Y, :] = v
            sent_rows[level][e, 0, pl.ds(x, 1), :] = v[:1]
            sent_rows[level][e, 1, pl.ds(x, 1), :] = v[Y - 1 :]
            return carry

        lax.fori_loop(0, X, plane, 0, unroll=4)
        start, finish, drain = exchange(
            p.at[e],
            X,
            Y,
            sent_rows[level].at[e],
            got_rows[level].at[e],
            3 + 4 * level + e,
            order,
        )
        start()
        drains.append(drain)
        finish()

    for level in range(LEVELS):
        X, Y = dims(level)
        produce(level, 0, lambda x, level=level: weight[level][x] * source[level][x])
        produce(level, 1, lambda x, level=level: sweep(level, 0, x))

        def restrict(x, carry, level=level, Y=Y):
            both = None
            for k in range(2):
                here, total = neighbour_sum(level, 1, 2 * x + k)
                left = (source[level][2 * x + k] - diag[level][2 * x + k] * here) + total
                both = left if both is None else both + left
            tmp[:Y, :] = both
            half = Y // 2
            summed = (
                tmp[pl.ds(0, half, stride=2), :] + tmp[pl.ds(1, half, stride=2), :]
            )
            summed = 0.5 * z_pair(summed, level)
            if level + 1 == LEVELS:
                gather_source[narrow, x] = summed
            else:
                source[level + 1][x] = summed
            return carry

        if level + 1 == LEVELS:
            for x in range(X // 2):
                restrict(x, 0)
        else:
            lax.fori_loop(0, X // 2, restrict, 0, unroll=4)

    source_start()
    face_finish()
    source_finish()
    X, Y = dims(LEVELS)
    step = 1 << LEVELS
    row = lax.broadcasted_iota(jnp.int32, (Y, Z), 0)
    col = lax.broadcasted_iota(jnp.int32, (Y, Z), 1)
    for n in range(n_narrow):
        for x in range(X):
            fxl, fxh = gather_faces[n, x], gather_faces[n, x + 1]
            fyl, fyh, fzl, fzh = (gather_faces[n, X + 1 + k * X + x] for k in range(4))
            total = ((fxl + fxh) + (fyl + fyh)) + (fzl + fzh)
            w = DAMPING / total
            at = n * X + x
            coef[0, at] = w * fxl
            coef[1, at] = w * fxh
            coef[2, at] = jnp.where(row == 0, 0.0, w * fyl)
            coef[3, at] = jnp.where(row == Y - 1, 0.0, w * fyh)
            coef[4, at] = jnp.where(col < step, 0.0, w * fzl)
            coef[5, at] = jnp.where(col >= Z - step, 0.0, w * fzh)
            coef[6, at] = w * gather_source[n, x]

    zero_plane = jnp.zeros((1, Y, Z), jnp.float32)

    def bottom(k, cur):
        new = KEEP * cur + coef[6]
        new += coef[0] * jnp.concatenate([zero_plane, cur[:-1]], axis=0)
        new += coef[1] * jnp.concatenate([cur[1:], zero_plane], axis=0)
        new += coef[2] * pltpu.roll(cur, 1, 1)
        new += coef[3] * pltpu.roll(cur, Y - 1, 1)
        new += coef[4] * pltpu.roll(cur, step, 2)
        new += coef[5] * pltpu.roll(cur, Z - step, 2)
        return new

    coef[7] = lax.fori_loop(0, BOTTOM - 1, bottom, coef[6], unroll=3)
    for x in range(X):
        answer[LEVELS][x] = coef[7, narrow * X + x]

    for level in reversed(range(LEVELS)):
        X, Y = dims(level)
        half = Y // 2

        def raised(x, level=level, Y=Y, half=half):
            e = answer[level + 1][x // 2]
            tmp[pl.ds(0, half, stride=2), :] = e
            tmp[pl.ds(1, half, stride=2), :] = e
            return iterates[level][1, x + 1, PAD : PAD + Y, :] + tmp[:Y, :]

        produce(level, 2, raised)
        produce(level, 3, lambda x, level=level: sweep(level, 2, x))
        target = out_ref if level == 0 else answer[level]

        def close(x, carry, level=level, target=target):
            target[x] = sweep(level, 3, x)
            return carry

        lax.fori_loop(0, X, close, 0, unroll=4)

    face_drain()
    source_drain()
    for drain in drains:
        drain()


def f32(*shape):
    return pltpu.VMEM(shape, jnp.float32)


def call_solve(n_wide, n_narrow, receive_index, arrived):
    X3, Y3 = dims(LEVELS)
    levels = [dims(level) for level in range(LEVELS)]
    padded = f32(X0 + 2, Y0 + 2 * PAD, Z)
    each = [f32(X, Y, Z) for X, Y in levels]
    moves = 3 + 4 * LEVELS
    scratch = [
        f32(64, Z),
        f32(Y0, Z),
        padded,
        padded,
        f32(X0, Y0, Z),
        padded,
        f32(2, 2, X0, Z),
        f32(2, 2, X0, Z),
        [f32(4, X + 2, Y + 2 * PAD, Z) for X, Y in levels],
        [f32(4, 2, X, Z) for X, Y in levels],
        [f32(4, 2, X, Z) for X, Y in levels],
        [f32(X + 1, Y, Z) for X, Y in levels],
        each,
        each,
        each,
        each,
        each,
        each,
        each,
        [f32(*dims(level), Z) for level in range(LEVELS + 1)],
        f32(n_narrow, 5 * X3 + 1, Y3, Z),
        f32(n_narrow, X3, Y3, Z),
        f32(8, n_narrow * X3, Y3, Z),
        pltpu.SemaphoreType.DMA((moves, 4)),
        pltpu.SemaphoreType.DMA((moves, 4)),
        pltpu.SemaphoreType.DMA((2, n_narrow - 1)),
        pltpu.SemaphoreType.DMA((2, n_narrow - 1)),
    ]
    return pl.pallas_call(
        functools.partial(solve_kernel, n_wide, n_narrow),
        out_shape=jax.ShapeDtypeStruct((X0, Y0, Z), jnp.float32),
        in_specs=[
            pl.BlockSpec(memory_space=pltpu.SMEM),
            pl.BlockSpec(memory_space=pltpu.VMEM),
        ],
        out_specs=pl.BlockSpec(memory_space=pltpu.VMEM),
        scratch_shapes=scratch,
        compiler_params=pltpu.CompilerParams(
            collective_id=0, has_side_effects=True, vmem_limit_bytes=VMEM_LIMIT
        ),
        cost_estimate=pl.CostEstimate(
            flops=200_000_000, bytes_accessed=200_000_000, transcendentals=0
        ),
    )(receive_index, arrived)


def shards(n_wide, n_narrow, target_slot, fields):
    per_owner, n_fields, cells = fields.shape
    owners = n_wide * n_narrow
    me = lax.axis_index("wide") * n_narrow + lax.axis_index("narrow")
    slots = owners * CAPACITY
    place = jnp.arange(per_owner, dtype=jnp.int32)
    own_target = lax.dynamic_slice_in_dim(target_slot, me * per_owner, per_owner) // per_owner
    earlier = jnp.sum(
        (
            (own_target[:, None] == own_target[None, :]) & (place[:, None] > place[None, :])
        ).astype(jnp.int32),
        axis=1,
    )
    own_slot = own_target * CAPACITY + earlier
    slot_ids = jnp.arange(slots, dtype=jnp.int32)
    send_index = jnp.sum(
        jnp.where(own_slot[None, :] == slot_ids[:, None], place[None, :], 0), axis=1
    )
    table = target_slot.reshape(owners, per_owner)
    to_me = table // per_owner == me
    rank = jnp.sum(
        (to_me[:, None, :] & (place[None, :, None] > place[None, None, :])).astype(jnp.int32),
        axis=2,
    )
    row = jnp.arange(owners, dtype=jnp.int32)[:, None] * CAPACITY + rank
    receive_index = jnp.sum(
        jnp.where(
            target_slot[None, :] == (me * per_owner + place)[:, None], row.reshape(-1)[None, :], 0
        ),
        axis=1,
    )

    smem = pl.BlockSpec(memory_space=pltpu.SMEM)
    vmem = pl.BlockSpec(memory_space=pltpu.VMEM)
    params = pltpu.CompilerParams(vmem_limit_bytes=VMEM_LIMIT)
    carried_fields = n_fields - SOLVED
    solved, carried = pl.pallas_call(
        pack_kernel,
        out_shape=(
            jax.ShapeDtypeStruct((slots, SOLVED, cells), fields.dtype),
            jax.ShapeDtypeStruct((slots, carried_fields, cells), fields.dtype),
        ),
        in_specs=[smem, vmem],
        out_specs=(vmem, vmem),
        compiler_params=params,
    )(send_index, fields)
    swap = functools.partial(
        lax.all_to_all,
        axis_name=("wide", "narrow"),
        split_axis=0,
        concat_axis=0,
        tiled=True,
    )
    solved = swap(solved)
    solved, carried = lax.optimization_barrier((solved, carried))
    carried = swap(carried)
    pressure = call_solve(n_wide, n_narrow, receive_index, solved)
    migrated = pl.pallas_call(
        merge_kernel,
        out_shape=jax.ShapeDtypeStruct(fields.shape, fields.dtype),
        in_specs=[smem, vmem, vmem],
        out_specs=vmem,
        compiler_params=params,
    )(receive_index, solved, carried)
    return migrated, pressure


def solution(mesh):
    body = functools.partial(shards, mesh.shape["wide"], mesh.shape["narrow"])
    in_specs = (P(), P(("wide", "narrow"), None, None))
    out_specs = (P(("wide", "narrow"), None, None), P("narrow", "wide", None))
    return jax.shard_map(body, mesh=mesh, in_specs=in_specs, out_specs=out_specs, check_vma=False)
```

```python
import functools

import jax
import jax.numpy as jnp
from jax import lax
from jax.experimental import pallas as pl
from jax.experimental.pallas import tpu as pltpu
from jax.sharding import PartitionSpec as P

PATCH = 16
BYP = 4
BZP = 8
LEVELS = 3
BOTTOM = 16
DAMPING = 0.8
KEEP = 1.0 - DAMPING
SOLVED = 4
CAPACITY = 2
X0 = PATCH
Y0 = PATCH * BYP
Z = PATCH * BZP
PAD = 8
MESH = pl.DeviceIdType.MESH
STRIDE = 13
SHARES = (4,) + (2,) * 14
VMEM_LIMIT = 60 * 1024 * 1024


def dims(level):
    return X0 >> level, Y0 >> level


def pack_kernel(index_ref, fields_ref, solved_ref, carried_ref):
    def one(slot, carry):
        patch = fields_ref[index_ref[slot]]
        solved_ref[slot] = patch[:SOLVED]
        carried_ref[slot] = patch[SOLVED:]
        return carry

    lax.fori_loop(0, solved_ref.shape[0], one, 0, unroll=4)


def merge_kernel(index_ref, solved_ref, carried_ref, out_ref):
    def one(patch, carry):
        row = index_ref[patch]
        out_ref[patch, :SOLVED] = solved_ref[row]
        out_ref[patch, SOLVED:] = carried_ref[row]
        return carry

    lax.fori_loop(0, out_ref.shape[0], one, 0, unroll=4)


def solve_kernel(
    n_wide,
    n_narrow,
    index_ref,
    arrived_ref,
    carried_ref,
    out_ref,
    moved_ref,
    turn,
    tmp,
    grid_u,
    grid_v,
    grid_w,
    grid_r,
    field_sent,
    field_got,
    iterates,
    sent_rows,
    got_rows,
    face_x,
    face_yl,
    face_yh,
    face_zl,
    face_zh,
    diag,
    weight,
    source,
    answer,
    gather_faces,
    gather_source,
    coef,
    send_sem,
    recv_sem,
    gsend_sem,
    grecv_sem,
    carry_send_sem,
    carry_recv_sem,
    own_sem,
):
    wide = lax.axis_index("wide")
    narrow = lax.axis_index("narrow")
    has = {
        "xl": narrow > 0,
        "xh": narrow < n_narrow - 1,
        "yl": wide > 0,
        "yh": wide < n_wide - 1,
    }
    peer = {
        "xl": (wide, narrow - 1),
        "xh": (wide, narrow + 1),
        "yl": (wide - 1, narrow),
        "yh": (wide + 1, narrow),
    }
    order = ("xl", "xh", "yl", "yh")
    others = [(wide, lax.rem(narrow + d, n_narrow)) for d in range(1, n_narrow)]

    barrier = pltpu.get_barrier_semaphore()
    owners = n_wide * n_narrow
    me = wide * n_narrow + narrow

    def owner_at(distance):
        owner = lax.rem(me + distance, owners)
        return owner, (owner // n_narrow, lax.rem(owner, n_narrow))

    def greet(d, carry):
        _, device = owner_at(d)
        pl.semaphore_signal(barrier, inc=1, device_id=device, device_id_type=MESH)
        return carry

    lax.fori_loop(1, owners, greet, 0)
    pl.semaphore_wait(barrier, owners - 1)

    def block(owner):
        return pl.ds(owner * CAPACITY, CAPACITY)

    def carry_copy(k):
        d = lax.rem(k * STRIDE, owners)
        owner, device = owner_at(d)
        return pltpu.make_async_remote_copy(
            src_ref=carried_ref.at[block(owner)],
            dst_ref=moved_ref.at[block(me)],
            send_sem=carry_send_sem.at[k],
            recv_sem=carry_recv_sem.at[k],
            device_id=device,
            device_id_type=MESH,
        )

    def carry_landing(k):
        d = lax.rem(k * STRIDE, owners)
        _, device = owner_at(d)
        came, _ = owner_at(owners - d)
        return pltpu.make_async_remote_copy(
            src_ref=carried_ref.at[block(me)],
            dst_ref=moved_ref.at[block(came)],
            send_sem=carry_send_sem.at[k],
            recv_sem=carry_recv_sem.at[k],
            device_id=device,
            device_id_type=MESH,
        )

    own_copy = pltpu.make_async_copy(
        carried_ref.at[block(me)], moved_ref.at[block(me)], own_sem
    )
    own_copy.start()
    shares = SHARES
    bounds = [
        1 + (owners - 1) * sum(shares[:k]) // sum(shares) for k in range(len(shares) + 1)
    ]
    pushed = []

    def push():
        turn_now = len(pushed)
        pushed.append(turn_now)

        def begin(k, carry):
            carry_copy(k).start()
            return carry

        lax.fori_loop(bounds[turn_now], bounds[turn_now + 1], begin, 0)

    push()

    lane = lax.broadcasted_iota(jnp.int32, (8, Z), 1)
    block_lane = lane // PATCH

    lower_bits = [(block_lane // s) % 2 == 1 for s in (1, 2, 4)]

    def to_grid(step, carry):
        b = step // X0
        i = step % X0
        at = pl.multiple_of(i * 2 * Z, 2 * Z)
        rows = []
        for c in range(BZP):
            both = arrived_ref[index_ref[b * BZP + c], :, pl.ds(at, 2 * Z)].astype(
                jnp.float32
            )
            rows.append(jnp.concatenate([both[:, :Z], both[:, Z:]], axis=0))
        for bit, s in zip(lower_bits, (1, 2, 4)):
            new = list(rows)
            for c in range(BZP):
                if c & s == 0:
                    low, high = rows[c], rows[c + s]
                    new[c] = jnp.where(bit, pltpu.roll(high, PATCH * s, 1), low)
                    new[c + s] = jnp.where(bit, high, pltpu.roll(low, Z - PATCH * s, 1))
            rows = new
        for j in range(8):
            turn[8 * j : 8 * j + 8, :] = rows[j]
        for half in range(2):
            y = pl.multiple_of(b * PATCH + half * 8, 8)
            for f, ref in enumerate((grid_u, grid_v, grid_w, grid_r)):
                values = turn[pl.ds(half * SOLVED + f, 8, stride=8), :]
                if f == 2:
                    ref[i, pl.ds(y, 8), :] = values
                else:
                    ref[i + 1, pl.ds(PAD + y, 8), :] = values
        return carry

    lax.fori_loop(0, BYP * X0, to_grid, 0, unroll=4)

    def exchange(padded, X, Y, sent, got, slot, sides):
        mid = pl.ds(PAD, Y)
        ends = {
            "xl": (lambda: padded.at[1, mid], lambda: padded.at[X + 1, mid]),
            "xh": (lambda: padded.at[X, mid], lambda: padded.at[0, mid]),
            "yl": (lambda: sent.at[0], lambda: got.at[1]),
            "yh": (lambda: sent.at[1], lambda: got.at[0]),
        }
        back = {"xl": "xh", "xh": "xl", "yl": "yh", "yh": "yl"}

        def copy(side):
            src, dst = ends[side]
            return pltpu.make_async_remote_copy(
                src_ref=src(),
                dst_ref=dst(),
                send_sem=send_sem.at[slot, order.index(side)],
                recv_sem=recv_sem.at[slot, order.index(back[side])],
                device_id=peer[side],
                device_id_type=MESH,
            )

        def landing(side):
            src, dst = ends[back[side]]
            return pltpu.make_async_remote_copy(
                src_ref=src(),
                dst_ref=dst(),
                send_sem=send_sem.at[slot, order.index(side)],
                recv_sem=recv_sem.at[slot, order.index(side)],
                device_id=peer[side],
                device_id_type=MESH,
            )

        def start():
            for side in sides:

                @pl.when(has[side])
                def _():
                    copy(side).start()

        def finish():
            for side in sides:

                @pl.when(has[side])
                def _():
                    landing(side).wait_recv()

                @pl.when(jnp.logical_not(has[side]))
                def _():
                    if side == "xl":
                        padded[0, PAD : PAD + Y, :] = jnp.zeros((Y, Z), jnp.float32)
                    elif side == "xh":
                        padded[X + 1, PAD : PAD + Y, :] = jnp.zeros((Y, Z), jnp.float32)
                    elif side == "yl":
                        got[0] = jnp.zeros((X, Z), jnp.float32)
                    else:
                        got[1] = jnp.zeros((X, Z), jnp.float32)

            if "yl" in sides:

                for x in range(X):
                    padded[x + 1, PAD - 1 : PAD, :] = got[0, x : x + 1, :]
                    padded[x + 1, PAD + Y : PAD + Y + 1, :] = got[1, x : x + 1, :]

        def drain():
            for side in sides:

                @pl.when(has[side])
                def _():
                    copy(side).wait_send()

        return start, finish, drain

    drains = []

    for k, ref in ((0, grid_v), (1, grid_r)):
        for x in range(X0):
            field_sent[k, 0, x : x + 1, :] = ref[x + 1, PAD : PAD + 1, :]
            field_sent[k, 1, x : x + 1, :] = ref[x + 1, PAD + Y0 - 1 : PAD + Y0, :]
    field_moves = [
        exchange(grid_r, X0, Y0, field_sent.at[1], field_got.at[1], 0, order),
        exchange(grid_u, X0, Y0, None, None, 1, ("xl", "xh")),
        exchange(grid_v, X0, Y0, field_sent.at[0], field_got.at[0], 2, ("yl", "yh")),
    ]
    for start, finish, drain in field_moves:
        start()
        drains.append(drain)
    push()
    for start, finish, drain in field_moves:
        finish()

    def z_low(values, step):
        rolled = pltpu.roll(values, step, 1)
        at = lax.broadcasted_iota(jnp.int32, values.shape, 1)
        return jnp.where(at < step, 0.0, rolled)

    def z_high(values, step):
        rolled = pltpu.roll(values, Z - step, 1)
        at = lax.broadcasted_iota(jnp.int32, values.shape, 1)
        return jnp.where(at >= Z - step, 0.0, rolled)

    mid0 = pl.ds(PAD, Y0)

    def first(x, carry):
        here = grid_r[x + 1, mid0, :]
        fxl = 2.0 / (grid_r[x, mid0, :] + here)
        fxh = 2.0 / (here + grid_r[x + 2, mid0, :])
        fyl = 2.0 / (grid_r[x + 1, PAD - 1 : PAD - 1 + Y0, :] + here)
        fyh = 2.0 / (grid_r[x + 1, PAD + 1 : PAD + 1 + Y0, :] + here)
        fzl = 2.0 / (z_low(here, 1) + here)
        fzh = 2.0 / (z_high(here, 1) + here)
        face_x[0][x] = fxl
        face_x[0][x + 1] = fxh
        face_yl[0][x] = fyl
        face_yh[0][x] = fyh
        face_zl[0][x] = fzl
        face_zh[0][x] = fzh
        total = ((fxl + fxh) + (fyl + fyh)) + (fzl + fzh)
        diag[0][x] = total
        weight[0][x] = DAMPING / total
        w = grid_w[x]
        du = grid_u[x + 2, mid0, :] - grid_u[x, mid0, :]
        dv = (
            grid_v[x + 1, PAD + 1 : PAD + 1 + Y0, :]
            - grid_v[x + 1, PAD - 1 : PAD - 1 + Y0, :]
        )
        source[0][x] = -0.5 * ((du + dv) + (z_high(w, 1) - z_low(w, 1)))
        return carry

    lax.fori_loop(0, X0, first, 0, unroll=4)

    def z_bit(shape, level):
        at = lax.broadcasted_iota(jnp.int32, shape, 1)
        return (at // (1 << level)) % 2 == 1

    def z_pair(values, level):
        step = 1 << level
        other = jnp.where(
            z_bit(values.shape, level),
            pltpu.roll(values, step, 1),
            pltpu.roll(values, Z - step, 1),
        )
        return values + other

    def z_even(values, level):
        step = 1 << level
        return jnp.where(
            z_bit(values.shape, level), pltpu.roll(values, step, 1), values
        )

    def z_odd(values, level):
        step = 1 << level
        return jnp.where(
            z_bit(values.shape, level), values, pltpu.roll(values, Z - step, 1)
        )

    for level in range(LEVELS):
        X, Y = dims(level + 1)
        even, odd = pl.ds(0, Y, stride=2), pl.ds(1, Y, stride=2)
        last = level + 1 == LEVELS

        def coarse_x(x, level=level, even=even, odd=odd):
            fx = face_x[level]
            return 0.25 * z_pair(fx[2 * x, even, :] + fx[2 * x, odd, :], level)

        def coarse_rest(x, level=level, even=even, odd=odd):
            yl, yh = face_yl[level], face_yh[level]
            zl, zh = face_zl[level], face_zh[level]
            fyl = 0.25 * z_pair(yl[2 * x, even, :] + yl[2 * x + 1, even, :], level)
            fyh = 0.25 * z_pair(yh[2 * x, odd, :] + yh[2 * x + 1, odd, :], level)
            four_l = (zl[2 * x, even, :] + zl[2 * x, odd, :]) + (
                zl[2 * x + 1, even, :] + zl[2 * x + 1, odd, :]
            )
            four_h = (zh[2 * x, even, :] + zh[2 * x, odd, :]) + (
                zh[2 * x + 1, even, :] + zh[2 * x + 1, odd, :]
            )
            return fyl, fyh, z_even(0.25 * four_l, level), z_odd(0.25 * four_h, level)

        if last:
            for x in range(X + 1):
                gather_faces[narrow, x] = coarse_x(x)
            for x in range(X):
                for k, face in enumerate(coarse_rest(x)):
                    gather_faces[narrow, X + 1 + k * X + x] = face
        else:

            def planes(x, carry, level=level, rest=coarse_rest, cx=coarse_x):
                fxl, fxh = cx(x), cx(x + 1)
                fyl, fyh, fzl, fzh = rest(x)
                face_x[level + 1][x] = fxl
                face_x[level + 1][x + 1] = fxh
                face_yl[level + 1][x] = fyl
                face_yh[level + 1][x] = fyh
                face_zl[level + 1][x] = fzl
                face_zh[level + 1][x] = fzh
                total = ((fxl + fxh) + (fyl + fyh)) + (fzl + fzh)
                diag[level + 1][x] = total
                weight[level + 1][x] = DAMPING / total
                return carry

            lax.fori_loop(0, X, planes, 0, unroll=4)

    def gather(ref, which):
        def copy(d):
            return pltpu.make_async_remote_copy(
                src_ref=ref.at[narrow],
                dst_ref=ref.at[narrow],
                send_sem=gsend_sem.at[which, d - 1],
                recv_sem=grecv_sem.at[which, d - 1],
                device_id=others[d - 1],
                device_id_type=MESH,
            )

        def landing(d):
            came = lax.rem(narrow + n_narrow - d, n_narrow)
            return pltpu.make_async_remote_copy(
                src_ref=ref.at[narrow],
                dst_ref=ref.at[came],
                send_sem=gsend_sem.at[which, d - 1],
                recv_sem=grecv_sem.at[which, d - 1],
                device_id=others[d - 1],
                device_id_type=MESH,
            )

        def start():
            for d in range(1, n_narrow):
                copy(d).start()

        def finish():
            for d in range(1, n_narrow):
                landing(d).wait_recv()

        def drain():
            for d in range(1, n_narrow):
                copy(d).wait_send()

        return start, finish, drain

    face_start, face_finish, face_drain = gather(gather_faces, 0)
    source_start, source_finish, source_drain = gather(gather_source, 1)
    face_start()

    def neighbour_sum(level, e, x):
        _, Y = dims(level)
        p = iterates[level]
        step = 1 << level
        mid = pl.ds(PAD, Y)
        here = p[e, x + 1, mid, :]
        total = (
            face_x[level][x] * p[e, x, mid, :]
            + face_x[level][x + 1] * p[e, x + 2, mid, :]
        )
        total += face_yl[level][x] * p[e, x + 1, PAD - 1 : PAD - 1 + Y, :]
        total += face_yh[level][x] * p[e, x + 1, PAD + 1 : PAD + 1 + Y, :]
        total += face_zl[level][x] * z_low(here, step)
        total += face_zh[level][x] * z_high(here, step)
        return here, total

    def sweep(level, e, x):
        here, total = neighbour_sum(level, e, x)
        return KEEP * here + weight[level][x] * (source[level][x] + total)

    def produce(level, e, values_of):
        X, Y = dims(level)
        p = iterates[level]

        def plane(x, carry):
            v = values_of(x)
            p[e, x + 1, PAD : PAD + Y, :] = v
            sent_rows[level][e, 0, pl.ds(x, 1), :] = v[:1]
            sent_rows[level][e, 1, pl.ds(x, 1), :] = v[Y - 1 :]
            return carry

        lax.fori_loop(0, X, plane, 0, unroll=4)
        start, finish, drain = exchange(
            p.at[e],
            X,
            Y,
            sent_rows[level].at[e],
            got_rows[level].at[e],
            3 + 4 * level + e,
            order,
        )
        start()
        drains.append(drain)
        push()
        finish()

    for level in range(LEVELS):
        X, Y = dims(level)
        produce(level, 0, lambda x, level=level: weight[level][x] * source[level][x])
        produce(level, 1, lambda x, level=level: sweep(level, 0, x))

        def restrict(x, carry, level=level, Y=Y):
            both = None
            for k in range(2):
                here, total = neighbour_sum(level, 1, 2 * x + k)
                left = (source[level][2 * x + k] - diag[level][2 * x + k] * here) + total
                both = left if both is None else both + left
            tmp[:Y, :] = both
            half = Y // 2
            summed = (
                tmp[pl.ds(0, half, stride=2), :] + tmp[pl.ds(1, half, stride=2), :]
            )
            summed = 0.5 * z_pair(summed, level)
            if level + 1 == LEVELS:
                gather_source[narrow, x] = summed
            else:
                source[level + 1][x] = summed
            return carry

        if level + 1 == LEVELS:
            for x in range(X // 2):
                restrict(x, 0)
        else:
            lax.fori_loop(0, X // 2, restrict, 0, unroll=4)

    source_start()
    push()
    face_finish()
    source_finish()
    X, Y = dims(LEVELS)
    step = 1 << LEVELS
    row = lax.broadcasted_iota(jnp.int32, (Y, Z), 0)
    col = lax.broadcasted_iota(jnp.int32, (Y, Z), 1)
    for n in range(n_narrow):
        for x in range(X):
            fxl, fxh = gather_faces[n, x], gather_faces[n, x + 1]
            fyl, fyh, fzl, fzh = (gather_faces[n, X + 1 + k * X + x] for k in range(4))
            total = ((fxl + fxh) + (fyl + fyh)) + (fzl + fzh)
            w = DAMPING / total
            at = n * X + x
            coef[0, at] = w * fxl
            coef[1, at] = w * fxh
            coef[2, at] = jnp.where(row == 0, 0.0, w * fyl)
            coef[3, at] = jnp.where(row == Y - 1, 0.0, w * fyh)
            coef[4, at] = jnp.where(col < step, 0.0, w * fzl)
            coef[5, at] = jnp.where(col >= Z - step, 0.0, w * fzh)
            coef[6, at] = w * gather_source[n, x]

    zero_plane = jnp.zeros((1, Y, Z), jnp.float32)

    def bottom(k, cur):
        new = KEEP * cur + coef[6]
        new += coef[0] * jnp.concatenate([zero_plane, cur[:-1]], axis=0)
        new += coef[1] * jnp.concatenate([cur[1:], zero_plane], axis=0)
        new += coef[2] * pltpu.roll(cur, 1, 1)
        new += coef[3] * pltpu.roll(cur, Y - 1, 1)
        new += coef[4] * pltpu.roll(cur, step, 2)
        new += coef[5] * pltpu.roll(cur, Z - step, 2)
        return new

    coef[7] = lax.fori_loop(0, BOTTOM - 1, bottom, coef[6], unroll=3)
    for x in range(X):
        answer[LEVELS][x] = coef[7, narrow * X + x]

    for level in reversed(range(LEVELS)):
        X, Y = dims(level)
        half = Y // 2

        def raised(x, level=level, Y=Y, half=half):
            e = answer[level + 1][x // 2]
            tmp[pl.ds(0, half, stride=2), :] = e
            tmp[pl.ds(1, half, stride=2), :] = e
            return iterates[level][1, x + 1, PAD : PAD + Y, :] + tmp[:Y, :]

        produce(level, 2, raised)
        produce(level, 3, lambda x, level=level: sweep(level, 2, x))
        target = out_ref if level == 0 else answer[level]

        def close(x, carry, level=level, target=target):
            target[x] = sweep(level, 3, x)
            return carry

        lax.fori_loop(0, X, close, 0, unroll=4)

    assert len(pushed) == len(shares)

    def end(k, carry):
        carry_landing(k).wait_recv()
        carry_copy(k).wait_send()
        return carry

    lax.fori_loop(1, owners, end, 0)
    own_copy.wait()
    face_drain()
    source_drain()
    for drain in drains:
        drain()


def f32(*shape):
    return pltpu.VMEM(shape, jnp.float32)


def call_solve(n_wide, n_narrow, receive_index, arrived, carried):
    X3, Y3 = dims(LEVELS)
    levels = [dims(level) for level in range(LEVELS)]
    padded = f32(X0 + 2, Y0 + 2 * PAD, Z)
    each = [f32(X, Y, Z) for X, Y in levels]
    moves = 3 + 4 * LEVELS
    scratch = [
        f32(64, Z),
        f32(Y0, Z),
        padded,
        padded,
        f32(X0, Y0, Z),
        padded,
        f32(2, 2, X0, Z),
        f32(2, 2, X0, Z),
        [f32(4, X + 2, Y + 2 * PAD, Z) for X, Y in levels],
        [f32(4, 2, X, Z) for X, Y in levels],
        [f32(4, 2, X, Z) for X, Y in levels],
        [f32(X + 1, Y, Z) for X, Y in levels],
        each,
        each,
        each,
        each,
        each,
        each,
        each,
        [f32(*dims(level), Z) for level in range(LEVELS + 1)],
        f32(n_narrow, 5 * X3 + 1, Y3, Z),
        f32(n_narrow, X3, Y3, Z),
        f32(8, n_narrow * X3, Y3, Z),
        pltpu.SemaphoreType.DMA((moves, 4)),
        pltpu.SemaphoreType.DMA((moves, 4)),
        pltpu.SemaphoreType.DMA((2, n_narrow - 1)),
        pltpu.SemaphoreType.DMA((2, n_narrow - 1)),
        pltpu.SemaphoreType.DMA((n_wide * n_narrow,)),
        pltpu.SemaphoreType.DMA((n_wide * n_narrow,)),
        pltpu.SemaphoreType.DMA,
    ]
    return pl.pallas_call(
        functools.partial(solve_kernel, n_wide, n_narrow),
        out_shape=(
            jax.ShapeDtypeStruct((X0, Y0, Z), jnp.float32),
            jax.ShapeDtypeStruct(carried.shape, carried.dtype),
        ),
        in_specs=[
            pl.BlockSpec(memory_space=pltpu.SMEM),
            pl.BlockSpec(memory_space=pltpu.VMEM),
            pl.BlockSpec(memory_space=pl.ANY),
        ],
        out_specs=(pl.BlockSpec(memory_space=pltpu.VMEM), pl.BlockSpec(memory_space=pl.ANY)),
        scratch_shapes=scratch,
        compiler_params=pltpu.CompilerParams(
            collective_id=0, has_side_effects=True, vmem_limit_bytes=VMEM_LIMIT
        ),
        cost_estimate=pl.CostEstimate(
            flops=200_000_000, bytes_accessed=200_000_000, transcendentals=0
        ),
    )(receive_index, arrived, carried)


def shards(n_wide, n_narrow, target_slot, fields):
    per_owner, n_fields, cells = fields.shape
    owners = n_wide * n_narrow
    me = lax.axis_index("wide") * n_narrow + lax.axis_index("narrow")
    slots = owners * CAPACITY
    place = jnp.arange(per_owner, dtype=jnp.int32)
    own_target = lax.dynamic_slice_in_dim(target_slot, me * per_owner, per_owner) // per_owner
    earlier = jnp.sum(
        (
            (own_target[:, None] == own_target[None, :]) & (place[:, None] > place[None, :])
        ).astype(jnp.int32),
        axis=1,
    )
    own_slot = own_target * CAPACITY + earlier
    slot_ids = jnp.arange(slots, dtype=jnp.int32)
    send_index = jnp.sum(
        jnp.where(own_slot[None, :] == slot_ids[:, None], place[None, :], 0), axis=1
    )
    table = target_slot.reshape(owners, per_owner)
    to_me = table // per_owner == me
    rank = jnp.sum(
        (to_me[:, None, :] & (place[None, :, None] > place[None, None, :])).astype(jnp.int32),
        axis=2,
    )
    row = jnp.arange(owners, dtype=jnp.int32)[:, None] * CAPACITY + rank
    receive_index = jnp.sum(
        jnp.where(
            target_slot[None, :] == (me * per_owner + place)[:, None], row.reshape(-1)[None, :], 0
        ),
        axis=1,
    )

    smem = pl.BlockSpec(memory_space=pltpu.SMEM)
    vmem = pl.BlockSpec(memory_space=pltpu.VMEM)
    params = pltpu.CompilerParams(vmem_limit_bytes=VMEM_LIMIT)
    carried_fields = n_fields - SOLVED
    solved, carried = pl.pallas_call(
        pack_kernel,
        out_shape=(
            jax.ShapeDtypeStruct((slots, SOLVED, cells), fields.dtype),
            jax.ShapeDtypeStruct((slots, carried_fields, cells), fields.dtype),
        ),
        in_specs=[smem, vmem],
        out_specs=(vmem, vmem),
        compiler_params=params,
    )(send_index, fields)
    swap = functools.partial(
        lax.all_to_all,
        axis_name=("wide", "narrow"),
        split_axis=0,
        concat_axis=0,
        tiled=True,
    )
    solved = swap(solved)
    pressure, carried = call_solve(n_wide, n_narrow, receive_index, solved, carried)
    migrated = pl.pallas_call(
        merge_kernel,
        out_shape=jax.ShapeDtypeStruct(fields.shape, fields.dtype),
        in_specs=[smem, vmem, vmem],
        out_specs=vmem,
        compiler_params=params,
    )(receive_index, solved, carried)
    return migrated, pressure


def solution(mesh):
    body = functools.partial(shards, mesh.shape["wide"], mesh.shape["narrow"])
    in_specs = (P(), P(("wide", "narrow"), None, None))
    out_specs = (P(("wide", "narrow"), None, None), P("narrow", "wide", None))
    return jax.shard_map(body, mesh=mesh, in_specs=in_specs, out_specs=out_specs, check_vma=False)
```

```python
import functools

import jax
import jax.numpy as jnp
from jax import lax
from jax.experimental import pallas as pl
from jax.experimental.pallas import tpu as pltpu
from jax.sharding import PartitionSpec as P

PATCH = 16
BYP = 4
BZP = 8
LEVELS = 3
BOTTOM = 16
DAMPING = 0.8
KEEP = 1.0 - DAMPING
SOLVED = 4
CAPACITY = 2
X0 = PATCH
Y0 = PATCH * BYP
Z = PATCH * BZP
PAD = 8
MESH = pl.DeviceIdType.MESH
STRIDE = 15
SHARES = (4,) + (2,) * 14
VMEM_LIMIT = 60 * 1024 * 1024


def dims(level):
    return X0 >> level, Y0 >> level


def pack_kernel(index_ref, fields_ref, solved_ref, carried_ref):
    def one(slot, carry):
        patch = fields_ref[index_ref[slot]]
        solved_ref[slot] = patch[:SOLVED]
        carried_ref[slot] = patch[SOLVED:]
        return carry

    lax.fori_loop(0, solved_ref.shape[0], one, 0, unroll=4)


def merge_kernel(index_ref, solved_ref, carried_ref, out_ref):
    def one(patch, carry):
        row = index_ref[patch]
        out_ref[patch, :SOLVED] = solved_ref[row]
        out_ref[patch, SOLVED:] = carried_ref[row]
        return carry

    lax.fori_loop(0, out_ref.shape[0], one, 0, unroll=4)


def solve_kernel(
    n_wide,
    n_narrow,
    index_ref,
    solved_ref,
    carried_ref,
    out_ref,
    arrived_ref,
    moved_ref,
    turn,
    tmp,
    grid_u,
    grid_v,
    grid_w,
    grid_r,
    field_sent,
    field_got,
    iterates,
    sent_rows,
    got_rows,
    face_x,
    face_yl,
    face_yh,
    face_zl,
    face_zh,
    diag,
    weight,
    source,
    answer,
    gather_faces,
    gather_source,
    coef,
    send_sem,
    recv_sem,
    gsend_sem,
    grecv_sem,
    carry_send_sem,
    carry_recv_sem,
    own_sem,
    solved_send_sem,
    solved_recv_sem,
):
    wide = lax.axis_index("wide")
    narrow = lax.axis_index("narrow")
    has = {
        "xl": narrow > 0,
        "xh": narrow < n_narrow - 1,
        "yl": wide > 0,
        "yh": wide < n_wide - 1,
    }
    peer = {
        "xl": (wide, narrow - 1),
        "xh": (wide, narrow + 1),
        "yl": (wide - 1, narrow),
        "yh": (wide + 1, narrow),
    }
    order = ("xl", "xh", "yl", "yh")
    others = [(wide, lax.rem(narrow + d, n_narrow)) for d in range(1, n_narrow)]

    barrier = pltpu.get_barrier_semaphore()
    owners = n_wide * n_narrow
    me = wide * n_narrow + narrow

    def owner_at(distance):
        owner = lax.rem(me + distance, owners)
        return owner, (owner // n_narrow, lax.rem(owner, n_narrow))

    def greet(d, carry):
        _, device = owner_at(d)
        pl.semaphore_signal(barrier, inc=1, device_id=device, device_id_type=MESH)
        return carry

    lax.fori_loop(1, owners, greet, 0)
    pl.semaphore_wait(barrier, owners - 1)

    def block(owner):
        return pl.ds(owner * CAPACITY, CAPACITY)

    def carry_copy(k):
        d = lax.rem(k * STRIDE, owners)
        owner, device = owner_at(d)
        return pltpu.make_async_remote_copy(
            src_ref=carried_ref.at[block(owner)],
            dst_ref=moved_ref.at[block(me)],
            send_sem=carry_send_sem.at[k],
            recv_sem=carry_recv_sem.at[k],
            device_id=device,
            device_id_type=MESH,
        )

    def carry_landing(k):
        d = lax.rem(k * STRIDE, owners)
        _, device = owner_at(d)
        came, _ = owner_at(owners - d)
        return pltpu.make_async_remote_copy(
            src_ref=carried_ref.at[block(me)],
            dst_ref=moved_ref.at[block(came)],
            send_sem=carry_send_sem.at[k],
            recv_sem=carry_recv_sem.at[k],
            device_id=device,
            device_id_type=MESH,
        )

    def solved_copy(k):
        d = lax.rem(k * STRIDE, owners)
        owner, device = owner_at(d)
        return pltpu.make_async_remote_copy(
            src_ref=solved_ref.at[block(owner)],
            dst_ref=arrived_ref.at[block(me)],
            send_sem=solved_send_sem.at[k],
            recv_sem=solved_recv_sem.at[k],
            device_id=device,
            device_id_type=MESH,
        )

    def solved_landing(k):
        d = lax.rem(k * STRIDE, owners)
        _, device = owner_at(d)
        came, _ = owner_at(owners - d)
        return pltpu.make_async_remote_copy(
            src_ref=solved_ref.at[block(me)],
            dst_ref=arrived_ref.at[block(came)],
            send_sem=solved_send_sem.at[k],
            recv_sem=solved_recv_sem.at[k],
            device_id=device,
            device_id_type=MESH,
        )

    def solved_begin(k, carry):
        solved_copy(k).start()
        return carry

    def solved_arrive(k, carry):
        solved_landing(k).wait_recv()
        return carry

    def solved_end(k, carry):
        solved_copy(k).wait_send()
        return carry

    lax.fori_loop(1, owners, solved_begin, 0)
    own_solved = pltpu.make_async_copy(
        solved_ref.at[block(me)], arrived_ref.at[block(me)], own_sem.at[1]
    )
    own_solved.start()
    own_copy = pltpu.make_async_copy(
        carried_ref.at[block(me)], moved_ref.at[block(me)], own_sem.at[0]
    )
    own_copy.start()
    shares = SHARES
    bounds = [
        1 + (owners - 1) * sum(shares[:k]) // sum(shares) for k in range(len(shares) + 1)
    ]
    pushed = []

    def push():
        turn_now = len(pushed)
        pushed.append(turn_now)

        def begin(k, carry):
            carry_copy(k).start()
            return carry

        lax.fori_loop(bounds[turn_now], bounds[turn_now + 1], begin, 0)

    own_solved.wait()
    lax.fori_loop(1, owners, solved_arrive, 0)
    push()

    lane = lax.broadcasted_iota(jnp.int32, (8, Z), 1)
    block_lane = lane // PATCH

    lower_bits = [(block_lane // s) % 2 == 1 for s in (1, 2, 4)]

    def to_grid(step, carry):
        b = step // X0
        i = step % X0
        at = pl.multiple_of(i * 2 * Z, 2 * Z)
        rows = []
        for c in range(BZP):
            both = arrived_ref[index_ref[b * BZP + c], :, pl.ds(at, 2 * Z)].astype(
                jnp.float32
            )
            rows.append(jnp.concatenate([both[:, :Z], both[:, Z:]], axis=0))
        for bit, s in zip(lower_bits, (1, 2, 4)):
            new = list(rows)
            for c in range(BZP):
                if c & s == 0:
                    low, high = rows[c], rows[c + s]
                    new[c] = jnp.where(bit, pltpu.roll(high, PATCH * s, 1), low)
                    new[c + s] = jnp.where(bit, high, pltpu.roll(low, Z - PATCH * s, 1))
            rows = new
        for j in range(8):
            turn[8 * j : 8 * j + 8, :] = rows[j]
        for half in range(2):
            y = pl.multiple_of(b * PATCH + half * 8, 8)
            for f, ref in enumerate((grid_u, grid_v, grid_w, grid_r)):
                values = turn[pl.ds(half * SOLVED + f, 8, stride=8), :]
                if f == 2:
                    ref[i, pl.ds(y, 8), :] = values
                else:
                    ref[i + 1, pl.ds(PAD + y, 8), :] = values
        return carry

    lax.fori_loop(0, BYP * X0, to_grid, 0, unroll=4)

    def exchange(padded, X, Y, sent, got, slot, sides):
        mid = pl.ds(PAD, Y)
        ends = {
            "xl": (lambda: padded.at[1, mid], lambda: padded.at[X + 1, mid]),
            "xh": (lambda: padded.at[X, mid], lambda: padded.at[0, mid]),
            "yl": (lambda: sent.at[0], lambda: got.at[1]),
            "yh": (lambda: sent.at[1], lambda: got.at[0]),
        }
        back = {"xl": "xh", "xh": "xl", "yl": "yh", "yh": "yl"}

        def copy(side):
            src, dst = ends[side]
            return pltpu.make_async_remote_copy(
                src_ref=src(),
                dst_ref=dst(),
                send_sem=send_sem.at[slot, order.index(side)],
                recv_sem=recv_sem.at[slot, order.index(back[side])],
                device_id=peer[side],
                device_id_type=MESH,
            )

        def landing(side):
            src, dst = ends[back[side]]
            return pltpu.make_async_remote_copy(
                src_ref=src(),
                dst_ref=dst(),
                send_sem=send_sem.at[slot, order.index(side)],
                recv_sem=recv_sem.at[slot, order.index(side)],
                device_id=peer[side],
                device_id_type=MESH,
            )

        def start():
            for side in sides:

                @pl.when(has[side])
                def _():
                    copy(side).start()

        def finish():
            for side in sides:

                @pl.when(has[side])
                def _():
                    landing(side).wait_recv()

                @pl.when(jnp.logical_not(has[side]))
                def _():
                    if side == "xl":
                        padded[0, PAD : PAD + Y, :] = jnp.zeros((Y, Z), jnp.float32)
                    elif side == "xh":
                        padded[X + 1, PAD : PAD + Y, :] = jnp.zeros((Y, Z), jnp.float32)
                    elif side == "yl":
                        got[0] = jnp.zeros((X, Z), jnp.float32)
                    else:
                        got[1] = jnp.zeros((X, Z), jnp.float32)

            if "yl" in sides:

                for x in range(X):
                    padded[x + 1, PAD - 1 : PAD, :] = got[0, x : x + 1, :]
                    padded[x + 1, PAD + Y : PAD + Y + 1, :] = got[1, x : x + 1, :]

        def drain():
            for side in sides:

                @pl.when(has[side])
                def _():
                    copy(side).wait_send()

        return start, finish, drain

    drains = []

    for k, ref in ((0, grid_v), (1, grid_r)):
        for x in range(X0):
            field_sent[k, 0, x : x + 1, :] = ref[x + 1, PAD : PAD + 1, :]
            field_sent[k, 1, x : x + 1, :] = ref[x + 1, PAD + Y0 - 1 : PAD + Y0, :]
    field_moves = [
        exchange(grid_r, X0, Y0, field_sent.at[1], field_got.at[1], 0, order),
        exchange(grid_u, X0, Y0, None, None, 1, ("xl", "xh")),
        exchange(grid_v, X0, Y0, field_sent.at[0], field_got.at[0], 2, ("yl", "yh")),
    ]
    for start, finish, drain in field_moves:
        start()
        drains.append(drain)
    push()
    for start, finish, drain in field_moves:
        finish()

    def z_low(values, step):
        rolled = pltpu.roll(values, step, 1)
        at = lax.broadcasted_iota(jnp.int32, values.shape, 1)
        return jnp.where(at < step, 0.0, rolled)

    def z_high(values, step):
        rolled = pltpu.roll(values, Z - step, 1)
        at = lax.broadcasted_iota(jnp.int32, values.shape, 1)
        return jnp.where(at >= Z - step, 0.0, rolled)

    mid0 = pl.ds(PAD, Y0)

    def first(x, carry):
        here = grid_r[x + 1, mid0, :]
        fxl = 2.0 / (grid_r[x, mid0, :] + here)
        fxh = 2.0 / (here + grid_r[x + 2, mid0, :])
        fyl = 2.0 / (grid_r[x + 1, PAD - 1 : PAD - 1 + Y0, :] + here)
        fyh = 2.0 / (grid_r[x + 1, PAD + 1 : PAD + 1 + Y0, :] + here)
        fzl = 2.0 / (z_low(here, 1) + here)
        fzh = 2.0 / (z_high(here, 1) + here)
        face_x[0][x] = fxl
        face_x[0][x + 1] = fxh
        face_yl[0][x] = fyl
        face_yh[0][x] = fyh
        face_zl[0][x] = fzl
        face_zh[0][x] = fzh
        total = ((fxl + fxh) + (fyl + fyh)) + (fzl + fzh)
        diag[0][x] = total
        weight[0][x] = DAMPING / total
        w = grid_w[x]
        du = grid_u[x + 2, mid0, :] - grid_u[x, mid0, :]
        dv = (
            grid_v[x + 1, PAD + 1 : PAD + 1 + Y0, :]
            - grid_v[x + 1, PAD - 1 : PAD - 1 + Y0, :]
        )
        source[0][x] = -0.5 * ((du + dv) + (z_high(w, 1) - z_low(w, 1)))
        return carry

    lax.fori_loop(0, X0, first, 0, unroll=4)

    def z_bit(shape, level):
        at = lax.broadcasted_iota(jnp.int32, shape, 1)
        return (at // (1 << level)) % 2 == 1

    def z_pair(values, level):
        step = 1 << level
        other = jnp.where(
            z_bit(values.shape, level),
            pltpu.roll(values, step, 1),
            pltpu.roll(values, Z - step, 1),
        )
        return values + other

    def z_even(values, level):
        step = 1 << level
        return jnp.where(
            z_bit(values.shape, level), pltpu.roll(values, step, 1), values
        )

    def z_odd(values, level):
        step = 1 << level
        return jnp.where(
            z_bit(values.shape, level), values, pltpu.roll(values, Z - step, 1)
        )

    for level in range(LEVELS):
        X, Y = dims(level + 1)
        even, odd = pl.ds(0, Y, stride=2), pl.ds(1, Y, stride=2)
        last = level + 1 == LEVELS

        def coarse_x(x, level=level, even=even, odd=odd):
            fx = face_x[level]
            return 0.25 * z_pair(fx[2 * x, even, :] + fx[2 * x, odd, :], level)

        def coarse_rest(x, level=level, even=even, odd=odd):
            yl, yh = face_yl[level], face_yh[level]
            zl, zh = face_zl[level], face_zh[level]
            fyl = 0.25 * z_pair(yl[2 * x, even, :] + yl[2 * x + 1, even, :], level)
            fyh = 0.25 * z_pair(yh[2 * x, odd, :] + yh[2 * x + 1, odd, :], level)
            four_l = (zl[2 * x, even, :] + zl[2 * x, odd, :]) + (
                zl[2 * x + 1, even, :] + zl[2 * x + 1, odd, :]
            )
            four_h = (zh[2 * x, even, :] + zh[2 * x, odd, :]) + (
                zh[2 * x + 1, even, :] + zh[2 * x + 1, odd, :]
            )
            return fyl, fyh, z_even(0.25 * four_l, level), z_odd(0.25 * four_h, level)

        if last:
            for x in range(X + 1):
                gather_faces[narrow, x] = coarse_x(x)
            for x in range(X):
                for k, face in enumerate(coarse_rest(x)):
                    gather_faces[narrow, X + 1 + k * X + x] = face
        else:

            def planes(x, carry, level=level, rest=coarse_rest, cx=coarse_x):
                fxl, fxh = cx(x), cx(x + 1)
                fyl, fyh, fzl, fzh = rest(x)
                face_x[level + 1][x] = fxl
                face_x[level + 1][x + 1] = fxh
                face_yl[level + 1][x] = fyl
                face_yh[level + 1][x] = fyh
                face_zl[level + 1][x] = fzl
                face_zh[level + 1][x] = fzh
                total = ((fxl + fxh) + (fyl + fyh)) + (fzl + fzh)
                diag[level + 1][x] = total
                weight[level + 1][x] = DAMPING / total
                return carry

            lax.fori_loop(0, X, planes, 0, unroll=4)

    def gather(ref, which):
        def copy(d):
            return pltpu.make_async_remote_copy(
                src_ref=ref.at[narrow],
                dst_ref=ref.at[narrow],
                send_sem=gsend_sem.at[which, d - 1],
                recv_sem=grecv_sem.at[which, d - 1],
                device_id=others[d - 1],
                device_id_type=MESH,
            )

        def landing(d):
            came = lax.rem(narrow + n_narrow - d, n_narrow)
            return pltpu.make_async_remote_copy(
                src_ref=ref.at[narrow],
                dst_ref=ref.at[came],
                send_sem=gsend_sem.at[which, d - 1],
                recv_sem=grecv_sem.at[which, d - 1],
                device_id=others[d - 1],
                device_id_type=MESH,
            )

        def start():
            for d in range(1, n_narrow):
                copy(d).start()

        def finish():
            for d in range(1, n_narrow):
                landing(d).wait_recv()

        def drain():
            for d in range(1, n_narrow):
                copy(d).wait_send()

        return start, finish, drain

    face_start, face_finish, face_drain = gather(gather_faces, 0)
    source_start, source_finish, source_drain = gather(gather_source, 1)
    face_start()

    def neighbour_sum(level, e, x):
        _, Y = dims(level)
        p = iterates[level]
        step = 1 << level
        mid = pl.ds(PAD, Y)
        here = p[e, x + 1, mid, :]
        total = (
            face_x[level][x] * p[e, x, mid, :]
            + face_x[level][x + 1] * p[e, x + 2, mid, :]
        )
        total += face_yl[level][x] * p[e, x + 1, PAD - 1 : PAD - 1 + Y, :]
        total += face_yh[level][x] * p[e, x + 1, PAD + 1 : PAD + 1 + Y, :]
        total += face_zl[level][x] * z_low(here, step)
        total += face_zh[level][x] * z_high(here, step)
        return here, total

    def sweep(level, e, x):
        here, total = neighbour_sum(level, e, x)
        return KEEP * here + weight[level][x] * (source[level][x] + total)

    def produce(level, e, values_of):
        X, Y = dims(level)
        p = iterates[level]

        def plane(x, carry):
            v = values_of(x)
            p[e, x + 1, PAD : PAD + Y, :] = v
            sent_rows[level][e, 0, pl.ds(x, 1), :] = v[:1]
            sent_rows[level][e, 1, pl.ds(x, 1), :] = v[Y - 1 :]
            return carry

        lax.fori_loop(0, X, plane, 0, unroll=4)
        start, finish, drain = exchange(
            p.at[e],
            X,
            Y,
            sent_rows[level].at[e],
            got_rows[level].at[e],
            3 + 4 * level + e,
            order,
        )
        start()
        drains.append(drain)
        push()
        finish()

    for level in range(LEVELS):
        X, Y = dims(level)
        produce(level, 0, lambda x, level=level: weight[level][x] * source[level][x])
        produce(level, 1, lambda x, level=level: sweep(level, 0, x))

        def restrict(x, carry, level=level, Y=Y):
            both = None
            for k in range(2):
                here, total = neighbour_sum(level, 1, 2 * x + k)
                left = (source[level][2 * x + k] - diag[level][2 * x + k] * here) + total
                both = left if both is None else both + left
            tmp[:Y, :] = both
            half = Y // 2
            summed = (
                tmp[pl.ds(0, half, stride=2), :] + tmp[pl.ds(1, half, stride=2), :]
            )
            summed = 0.5 * z_pair(summed, level)
            if level + 1 == LEVELS:
                gather_source[narrow, x] = summed
            else:
                source[level + 1][x] = summed
            return carry

        if level + 1 == LEVELS:
            for x in range(X // 2):
                restrict(x, 0)
        else:
            lax.fori_loop(0, X // 2, restrict, 0, unroll=4)

    source_start()
    push()
    face_finish()
    source_finish()
    X, Y = dims(LEVELS)
    step = 1 << LEVELS
    row = lax.broadcasted_iota(jnp.int32, (Y, Z), 0)
    col = lax.broadcasted_iota(jnp.int32, (Y, Z), 1)
    for n in range(n_narrow):
        for x in range(X):
            fxl, fxh = gather_faces[n, x], gather_faces[n, x + 1]
            fyl, fyh, fzl, fzh = (gather_faces[n, X + 1 + k * X + x] for k in range(4))
            total = ((fxl + fxh) + (fyl + fyh)) + (fzl + fzh)
            w = DAMPING / total
            at = n * X + x
            coef[0, at] = w * fxl
            coef[1, at] = w * fxh
            coef[2, at] = jnp.where(row == 0, 0.0, w * fyl)
            coef[3, at] = jnp.where(row == Y - 1, 0.0, w * fyh)
            coef[4, at] = jnp.where(col < step, 0.0, w * fzl)
            coef[5, at] = jnp.where(col >= Z - step, 0.0, w * fzh)
            coef[6, at] = w * gather_source[n, x]

    zero_plane = jnp.zeros((1, Y, Z), jnp.float32)

    def bottom(k, cur):
        new = KEEP * cur + coef[6]
        new += coef[0] * jnp.concatenate([zero_plane, cur[:-1]], axis=0)
        new += coef[1] * jnp.concatenate([cur[1:], zero_plane], axis=0)
        new += coef[2] * pltpu.roll(cur, 1, 1)
        new += coef[3] * pltpu.roll(cur, Y - 1, 1)
        new += coef[4] * pltpu.roll(cur, step, 2)
        new += coef[5] * pltpu.roll(cur, Z - step, 2)
        return new

    coef[7] = lax.fori_loop(0, BOTTOM - 1, bottom, coef[6], unroll=3)
    for x in range(X):
        answer[LEVELS][x] = coef[7, narrow * X + x]

    for level in reversed(range(LEVELS)):
        X, Y = dims(level)
        half = Y // 2

        def raised(x, level=level, Y=Y, half=half):
            e = answer[level + 1][x // 2]
            tmp[pl.ds(0, half, stride=2), :] = e
            tmp[pl.ds(1, half, stride=2), :] = e
            return iterates[level][1, x + 1, PAD : PAD + Y, :] + tmp[:Y, :]

        produce(level, 2, raised)
        produce(level, 3, lambda x, level=level: sweep(level, 2, x))
        target = out_ref if level == 0 else answer[level]

        def close(x, carry, level=level, target=target):
            target[x] = sweep(level, 3, x)
            return carry

        lax.fori_loop(0, X, close, 0, unroll=4)

    assert len(pushed) == len(shares)

    def end(k, carry):
        carry_landing(k).wait_recv()
        carry_copy(k).wait_send()
        return carry

    lax.fori_loop(1, owners, end, 0)
    lax.fori_loop(1, owners, solved_end, 0)
    own_copy.wait()
    face_drain()
    source_drain()
    for drain in drains:
        drain()


def f32(*shape):
    return pltpu.VMEM(shape, jnp.float32)


def call_solve(n_wide, n_narrow, receive_index, solved, carried):
    X3, Y3 = dims(LEVELS)
    levels = [dims(level) for level in range(LEVELS)]
    padded = f32(X0 + 2, Y0 + 2 * PAD, Z)
    each = [f32(X, Y, Z) for X, Y in levels]
    moves = 3 + 4 * LEVELS
    scratch = [
        f32(64, Z),
        f32(Y0, Z),
        padded,
        padded,
        f32(X0, Y0, Z),
        padded,
        f32(2, 2, X0, Z),
        f32(2, 2, X0, Z),
        [f32(4, X + 2, Y + 2 * PAD, Z) for X, Y in levels],
        [f32(4, 2, X, Z) for X, Y in levels],
        [f32(4, 2, X, Z) for X, Y in levels],
        [f32(X + 1, Y, Z) for X, Y in levels],
        each,
        each,
        each,
        each,
        each,
        each,
        each,
        [f32(*dims(level), Z) for level in range(LEVELS + 1)],
        f32(n_narrow, 5 * X3 + 1, Y3, Z),
        f32(n_narrow, X3, Y3, Z),
        f32(8, n_narrow * X3, Y3, Z),
        pltpu.SemaphoreType.DMA((moves, 4)),
        pltpu.SemaphoreType.DMA((moves, 4)),
        pltpu.SemaphoreType.DMA((2, n_narrow - 1)),
        pltpu.SemaphoreType.DMA((2, n_narrow - 1)),
        pltpu.SemaphoreType.DMA((n_wide * n_narrow,)),
        pltpu.SemaphoreType.DMA((n_wide * n_narrow,)),
        pltpu.SemaphoreType.DMA((2,)),
        pltpu.SemaphoreType.DMA((n_wide * n_narrow,)),
        pltpu.SemaphoreType.DMA((n_wide * n_narrow,)),
    ]
    return pl.pallas_call(
        functools.partial(solve_kernel, n_wide, n_narrow),
        out_shape=(
            jax.ShapeDtypeStruct((X0, Y0, Z), jnp.float32),
            jax.ShapeDtypeStruct(solved.shape, solved.dtype),
            jax.ShapeDtypeStruct(carried.shape, carried.dtype),
        ),
        in_specs=[
            pl.BlockSpec(memory_space=pltpu.SMEM),
            pl.BlockSpec(memory_space=pl.ANY),
            pl.BlockSpec(memory_space=pl.ANY),
        ],
        out_specs=(
            pl.BlockSpec(memory_space=pltpu.VMEM),
            pl.BlockSpec(memory_space=pltpu.VMEM),
            pl.BlockSpec(memory_space=pl.ANY),
        ),
        scratch_shapes=scratch,
        compiler_params=pltpu.CompilerParams(
            collective_id=0, has_side_effects=True, vmem_limit_bytes=VMEM_LIMIT
        ),
        cost_estimate=pl.CostEstimate(
            flops=200_000_000, bytes_accessed=200_000_000, transcendentals=0
        ),
    )(receive_index, solved, carried)


def shards(n_wide, n_narrow, target_slot, fields):
    per_owner, n_fields, cells = fields.shape
    owners = n_wide * n_narrow
    me = lax.axis_index("wide") * n_narrow + lax.axis_index("narrow")
    slots = owners * CAPACITY
    place = jnp.arange(per_owner, dtype=jnp.int32)
    own_target = lax.dynamic_slice_in_dim(target_slot, me * per_owner, per_owner) // per_owner
    earlier = jnp.sum(
        (
            (own_target[:, None] == own_target[None, :]) & (place[:, None] > place[None, :])
        ).astype(jnp.int32),
        axis=1,
    )
    own_slot = own_target * CAPACITY + earlier
    slot_ids = jnp.arange(slots, dtype=jnp.int32)
    send_index = jnp.sum(
        jnp.where(own_slot[None, :] == slot_ids[:, None], place[None, :], 0), axis=1
    )
    table = target_slot.reshape(owners, per_owner)
    to_me = table // per_owner == me
    rank = jnp.sum(
        (to_me[:, None, :] & (place[None, :, None] > place[None, None, :])).astype(jnp.int32),
        axis=2,
    )
    row = jnp.arange(owners, dtype=jnp.int32)[:, None] * CAPACITY + rank
    receive_index = jnp.sum(
        jnp.where(
            target_slot[None, :] == (me * per_owner + place)[:, None], row.reshape(-1)[None, :], 0
        ),
        axis=1,
    )

    smem = pl.BlockSpec(memory_space=pltpu.SMEM)
    vmem = pl.BlockSpec(memory_space=pltpu.VMEM)
    params = pltpu.CompilerParams(vmem_limit_bytes=VMEM_LIMIT)
    carried_fields = n_fields - SOLVED
    solved, carried = pl.pallas_call(
        pack_kernel,
        out_shape=(
            jax.ShapeDtypeStruct((slots, SOLVED, cells), fields.dtype),
            jax.ShapeDtypeStruct((slots, carried_fields, cells), fields.dtype),
        ),
        in_specs=[smem, vmem],
        out_specs=(vmem, vmem),
        compiler_params=params,
    )(send_index, fields)
    pressure, solved, carried = call_solve(n_wide, n_narrow, receive_index, solved, carried)
    migrated = pl.pallas_call(
        merge_kernel,
        out_shape=jax.ShapeDtypeStruct(fields.shape, fields.dtype),
        in_specs=[smem, vmem, vmem],
        out_specs=vmem,
        compiler_params=params,
    )(receive_index, solved, carried)
    return migrated, pressure


def solution(mesh):
    body = functools.partial(shards, mesh.shape["wide"], mesh.shape["narrow"])
    in_specs = (P(), P(("wide", "narrow"), None, None))
    out_specs = (P(("wide", "narrow"), None, None), P("narrow", "wide", None))
    return jax.shard_map(body, mesh=mesh, in_specs=in_specs, out_specs=out_specs, check_vma=False)
```

```python
import functools

import jax
import jax.numpy as jnp
from jax import lax
from jax.experimental import pallas as pl
from jax.experimental.pallas import tpu as pltpu
from jax.sharding import PartitionSpec as P

PATCH = 16
BYP = 4
BZP = 8
LEVELS = 3
BOTTOM = 16
DAMPING = 0.8
KEEP = 1.0 - DAMPING
SOLVED = 4
CAPACITY = 2
X0 = PATCH
Y0 = PATCH * BYP
Z = PATCH * BZP
PAD = 8
MESH = pl.DeviceIdType.MESH
STRIDE = 15
SHARES = (4, 3, 3) + (2,) * 10 + (1, 0)
VMEM_LIMIT = 60 * 1024 * 1024


def dims(level):
    return X0 >> level, Y0 >> level


def pack_kernel(index_ref, fields_ref, solved_ref, carried_ref):
    def one(slot, carry):
        patch = fields_ref[index_ref[slot]]
        solved_ref[slot] = patch[:SOLVED]
        carried_ref[slot] = patch[SOLVED:]
        return carry

    lax.fori_loop(0, solved_ref.shape[0], one, 0, unroll=8)


def merge_kernel(index_ref, solved_ref, carried_ref, out_ref):
    def one(patch, carry):
        row = index_ref[patch]
        out_ref[patch, :SOLVED] = solved_ref[row]
        out_ref[patch, SOLVED:] = carried_ref[row]
        return carry

    lax.fori_loop(0, out_ref.shape[0], one, 0, unroll=8)


def solve_kernel(
    n_wide,
    n_narrow,
    index_ref,
    solved_ref,
    carried_ref,
    out_ref,
    arrived_ref,
    moved_ref,
    turn,
    tmp,
    grid_u,
    grid_v,
    grid_w,
    grid_r,
    field_sent,
    field_got,
    iterates,
    sent_rows,
    got_rows,
    face_x,
    face_yl,
    face_yh,
    face_zl,
    face_zh,
    diag,
    weight,
    source,
    answer,
    gather_faces,
    gather_source,
    coef,
    send_sem,
    recv_sem,
    gsend_sem,
    grecv_sem,
    carry_send_sem,
    carry_recv_sem,
    own_sem,
    solved_send_sem,
    solved_recv_sem,
):
    wide = lax.axis_index("wide")
    narrow = lax.axis_index("narrow")
    has = {
        "xl": narrow > 0,
        "xh": narrow < n_narrow - 1,
        "yl": wide > 0,
        "yh": wide < n_wide - 1,
    }
    peer = {
        "xl": (wide, narrow - 1),
        "xh": (wide, narrow + 1),
        "yl": (wide - 1, narrow),
        "yh": (wide + 1, narrow),
    }
    order = ("xl", "xh", "yl", "yh")
    others = [(wide, lax.rem(narrow + d, n_narrow)) for d in range(1, n_narrow)]

    barrier = pltpu.get_barrier_semaphore()
    owners = n_wide * n_narrow
    me = wide * n_narrow + narrow

    def owner_at(distance):
        owner = lax.rem(me + distance, owners)
        return owner, (owner // n_narrow, lax.rem(owner, n_narrow))

    def greet(d, carry):
        _, device = owner_at(d)
        pl.semaphore_signal(barrier, inc=1, device_id=device, device_id_type=MESH)
        return carry

    lax.fori_loop(1, owners, greet, 0)
    pl.semaphore_wait(barrier, owners - 1)

    def block(owner):
        return pl.ds(owner * CAPACITY, CAPACITY)

    def carry_copy(k):
        d = lax.rem(k * STRIDE, owners)
        owner, device = owner_at(d)
        return pltpu.make_async_remote_copy(
            src_ref=carried_ref.at[block(owner)],
            dst_ref=moved_ref.at[block(me)],
            send_sem=carry_send_sem.at[k],
            recv_sem=carry_recv_sem.at[k],
            device_id=device,
            device_id_type=MESH,
        )

    def carry_landing(k):
        d = lax.rem(k * STRIDE, owners)
        _, device = owner_at(d)
        came, _ = owner_at(owners - d)
        return pltpu.make_async_remote_copy(
            src_ref=carried_ref.at[block(me)],
            dst_ref=moved_ref.at[block(came)],
            send_sem=carry_send_sem.at[k],
            recv_sem=carry_recv_sem.at[k],
            device_id=device,
            device_id_type=MESH,
        )

    def solved_copy(k):
        d = lax.rem(k * STRIDE, owners)
        owner, device = owner_at(d)
        return pltpu.make_async_remote_copy(
            src_ref=solved_ref.at[block(owner)],
            dst_ref=arrived_ref.at[block(me)],
            send_sem=solved_send_sem.at[k],
            recv_sem=solved_recv_sem.at[k],
            device_id=device,
            device_id_type=MESH,
        )

    def solved_landing(k):
        d = lax.rem(k * STRIDE, owners)
        _, device = owner_at(d)
        came, _ = owner_at(owners - d)
        return pltpu.make_async_remote_copy(
            src_ref=solved_ref.at[block(me)],
            dst_ref=arrived_ref.at[block(came)],
            send_sem=solved_send_sem.at[k],
            recv_sem=solved_recv_sem.at[k],
            device_id=device,
            device_id_type=MESH,
        )

    def solved_begin(k, carry):
        solved_copy(k).start()
        return carry

    def solved_arrive(k, carry):
        solved_landing(k).wait_recv()
        return carry

    def solved_end(k, carry):
        solved_copy(k).wait_send()
        return carry

    lax.fori_loop(1, owners, solved_begin, 0)
    own_solved = pltpu.make_async_copy(
        solved_ref.at[block(me)], arrived_ref.at[block(me)], own_sem.at[1]
    )
    own_solved.start()
    own_copy = pltpu.make_async_copy(
        carried_ref.at[block(me)], moved_ref.at[block(me)], own_sem.at[0]
    )
    own_copy.start()
    shares = SHARES
    bounds = [
        1 + (owners - 1) * sum(shares[:k]) // sum(shares) for k in range(len(shares) + 1)
    ]
    pushed = []

    def push():
        turn_now = len(pushed)
        pushed.append(turn_now)

        def begin(k, carry):
            carry_copy(k).start()
            return carry

        lax.fori_loop(bounds[turn_now], bounds[turn_now + 1], begin, 0)

    own_solved.wait()
    lax.fori_loop(1, owners, solved_arrive, 0)
    push()

    lane = lax.broadcasted_iota(jnp.int32, (8, Z), 1)
    block_lane = lane // PATCH

    lower_bits = [(block_lane // s) % 2 == 1 for s in (1, 2, 4)]

    def to_grid(step, carry):
        b = step // X0
        i = step % X0
        at = pl.multiple_of(i * 2 * Z, 2 * Z)
        rows = []
        for c in range(BZP):
            both = arrived_ref[index_ref[b * BZP + c], :, pl.ds(at, 2 * Z)].astype(
                jnp.float32
            )
            rows.append(jnp.concatenate([both[:, :Z], both[:, Z:]], axis=0))
        for bit, s in zip(lower_bits, (1, 2, 4)):
            new = list(rows)
            for c in range(BZP):
                if c & s == 0:
                    low, high = rows[c], rows[c + s]
                    new[c] = jnp.where(bit, pltpu.roll(high, PATCH * s, 1), low)
                    new[c + s] = jnp.where(bit, high, pltpu.roll(low, Z - PATCH * s, 1))
            rows = new
        for j in range(8):
            turn[8 * j : 8 * j + 8, :] = rows[j]
        for half in range(2):
            y = pl.multiple_of(b * PATCH + half * 8, 8)
            for f, ref in enumerate((grid_u, grid_v, grid_w, grid_r)):
                values = turn[pl.ds(half * SOLVED + f, 8, stride=8), :]
                if f == 2:
                    ref[i, pl.ds(y, 8), :] = values
                else:
                    ref[i + 1, pl.ds(PAD + y, 8), :] = values
        return carry

    lax.fori_loop(0, BYP * X0, to_grid, 0, unroll=8)

    def exchange(padded, X, Y, sent, got, slot, sides):
        mid = pl.ds(PAD, Y)
        ends = {
            "xl": (lambda: padded.at[1, mid], lambda: padded.at[X + 1, mid]),
            "xh": (lambda: padded.at[X, mid], lambda: padded.at[0, mid]),
            "yl": (lambda: sent.at[0], lambda: got.at[1]),
            "yh": (lambda: sent.at[1], lambda: got.at[0]),
        }
        back = {"xl": "xh", "xh": "xl", "yl": "yh", "yh": "yl"}

        def copy(side):
            src, dst = ends[side]
            return pltpu.make_async_remote_copy(
                src_ref=src(),
                dst_ref=dst(),
                send_sem=send_sem.at[slot, order.index(side)],
                recv_sem=recv_sem.at[slot, order.index(back[side])],
                device_id=peer[side],
                device_id_type=MESH,
            )

        def landing(side):
            src, dst = ends[back[side]]
            return pltpu.make_async_remote_copy(
                src_ref=src(),
                dst_ref=dst(),
                send_sem=send_sem.at[slot, order.index(side)],
                recv_sem=recv_sem.at[slot, order.index(side)],
                device_id=peer[side],
                device_id_type=MESH,
            )

        def start():
            for side in sides:

                @pl.when(has[side])
                def _():
                    copy(side).start()

        def finish():
            for side in sides:

                @pl.when(has[side])
                def _():
                    landing(side).wait_recv()

                @pl.when(jnp.logical_not(has[side]))
                def _():
                    if side == "xl":
                        padded[0, PAD : PAD + Y, :] = jnp.zeros((Y, Z), jnp.float32)
                    elif side == "xh":
                        padded[X + 1, PAD : PAD + Y, :] = jnp.zeros((Y, Z), jnp.float32)
                    elif side == "yl":
                        got[0] = jnp.zeros((X, Z), jnp.float32)
                    else:
                        got[1] = jnp.zeros((X, Z), jnp.float32)

            if "yl" in sides:

                for x in range(X):
                    padded[x + 1, PAD - 1 : PAD, :] = got[0, x : x + 1, :]
                    padded[x + 1, PAD + Y : PAD + Y + 1, :] = got[1, x : x + 1, :]

        def drain():
            for side in sides:

                @pl.when(has[side])
                def _():
                    copy(side).wait_send()

        return start, finish, drain

    drains = []

    for k, ref in ((0, grid_v), (1, grid_r)):
        for x in range(X0):
            field_sent[k, 0, x : x + 1, :] = ref[x + 1, PAD : PAD + 1, :]
            field_sent[k, 1, x : x + 1, :] = ref[x + 1, PAD + Y0 - 1 : PAD + Y0, :]
    field_moves = [
        exchange(grid_r, X0, Y0, field_sent.at[1], field_got.at[1], 0, order),
        exchange(grid_u, X0, Y0, None, None, 1, ("xl", "xh")),
        exchange(grid_v, X0, Y0, field_sent.at[0], field_got.at[0], 2, ("yl", "yh")),
    ]
    for start, finish, drain in field_moves:
        start()
        drains.append(drain)
    push()
    for start, finish, drain in field_moves:
        finish()

    def z_low(values, step):
        rolled = pltpu.roll(values, step, 1)
        at = lax.broadcasted_iota(jnp.int32, values.shape, 1)
        return jnp.where(at < step, 0.0, rolled)

    def z_high(values, step):
        rolled = pltpu.roll(values, Z - step, 1)
        at = lax.broadcasted_iota(jnp.int32, values.shape, 1)
        return jnp.where(at >= Z - step, 0.0, rolled)

    mid0 = pl.ds(PAD, Y0)

    def first(x, carry):
        here = grid_r[x + 1, mid0, :]
        fxl = 2.0 / (grid_r[x, mid0, :] + here)
        fxh = 2.0 / (here + grid_r[x + 2, mid0, :])
        fyl = 2.0 / (grid_r[x + 1, PAD - 1 : PAD - 1 + Y0, :] + here)
        fyh = 2.0 / (grid_r[x + 1, PAD + 1 : PAD + 1 + Y0, :] + here)
        fzl = 2.0 / (z_low(here, 1) + here)
        fzh = 2.0 / (z_high(here, 1) + here)
        face_x[0][x] = fxl
        face_x[0][x + 1] = fxh
        face_yl[0][x] = fyl
        face_yh[0][x] = fyh
        face_zl[0][x] = fzl
        face_zh[0][x] = fzh
        total = ((fxl + fxh) + (fyl + fyh)) + (fzl + fzh)
        diag[0][x] = total
        weight[0][x] = DAMPING / total
        w = grid_w[x]
        du = grid_u[x + 2, mid0, :] - grid_u[x, mid0, :]
        dv = (
            grid_v[x + 1, PAD + 1 : PAD + 1 + Y0, :]
            - grid_v[x + 1, PAD - 1 : PAD - 1 + Y0, :]
        )
        source[0][x] = -0.5 * ((du + dv) + (z_high(w, 1) - z_low(w, 1)))
        return carry

    lax.fori_loop(0, X0, first, 0, unroll=4)

    def z_bit(shape, level):
        at = lax.broadcasted_iota(jnp.int32, shape, 1)
        return (at // (1 << level)) % 2 == 1

    def z_pair(values, level):
        step = 1 << level
        other = jnp.where(
            z_bit(values.shape, level),
            pltpu.roll(values, step, 1),
            pltpu.roll(values, Z - step, 1),
        )
        return values + other

    def z_even(values, level):
        step = 1 << level
        return jnp.where(
            z_bit(values.shape, level), pltpu.roll(values, step, 1), values
        )

    def z_odd(values, level):
        step = 1 << level
        return jnp.where(
            z_bit(values.shape, level), values, pltpu.roll(values, Z - step, 1)
        )

    for level in range(LEVELS):
        X, Y = dims(level + 1)
        even, odd = pl.ds(0, Y, stride=2), pl.ds(1, Y, stride=2)
        last = level + 1 == LEVELS

        def coarse_x(x, level=level, even=even, odd=odd):
            fx = face_x[level]
            return 0.25 * z_pair(fx[2 * x, even, :] + fx[2 * x, odd, :], level)

        def coarse_rest(x, level=level, even=even, odd=odd):
            yl, yh = face_yl[level], face_yh[level]
            zl, zh = face_zl[level], face_zh[level]
            fyl = 0.25 * z_pair(yl[2 * x, even, :] + yl[2 * x + 1, even, :], level)
            fyh = 0.25 * z_pair(yh[2 * x, odd, :] + yh[2 * x + 1, odd, :], level)
            four_l = (zl[2 * x, even, :] + zl[2 * x, odd, :]) + (
                zl[2 * x + 1, even, :] + zl[2 * x + 1, odd, :]
            )
            four_h = (zh[2 * x, even, :] + zh[2 * x, odd, :]) + (
                zh[2 * x + 1, even, :] + zh[2 * x + 1, odd, :]
            )
            return fyl, fyh, z_even(0.25 * four_l, level), z_odd(0.25 * four_h, level)

        if last:
            for x in range(X + 1):
                gather_faces[narrow, x] = coarse_x(x)
            for x in range(X):
                for k, face in enumerate(coarse_rest(x)):
                    gather_faces[narrow, X + 1 + k * X + x] = face
        else:

            def planes(x, carry, level=level, rest=coarse_rest, cx=coarse_x):
                fxl, fxh = cx(x), cx(x + 1)
                fyl, fyh, fzl, fzh = rest(x)
                face_x[level + 1][x] = fxl
                face_x[level + 1][x + 1] = fxh
                face_yl[level + 1][x] = fyl
                face_yh[level + 1][x] = fyh
                face_zl[level + 1][x] = fzl
                face_zh[level + 1][x] = fzh
                total = ((fxl + fxh) + (fyl + fyh)) + (fzl + fzh)
                diag[level + 1][x] = total
                weight[level + 1][x] = DAMPING / total
                return carry

            lax.fori_loop(0, X, planes, 0, unroll=4)

    def gather(ref, which):
        def copy(d):
            return pltpu.make_async_remote_copy(
                src_ref=ref.at[narrow],
                dst_ref=ref.at[narrow],
                send_sem=gsend_sem.at[which, d - 1],
                recv_sem=grecv_sem.at[which, d - 1],
                device_id=others[d - 1],
                device_id_type=MESH,
            )

        def landing(d):
            came = lax.rem(narrow + n_narrow - d, n_narrow)
            return pltpu.make_async_remote_copy(
                src_ref=ref.at[narrow],
                dst_ref=ref.at[came],
                send_sem=gsend_sem.at[which, d - 1],
                recv_sem=grecv_sem.at[which, d - 1],
                device_id=others[d - 1],
                device_id_type=MESH,
            )

        def start():
            for d in range(1, n_narrow):
                copy(d).start()

        def finish():
            for d in range(1, n_narrow):
                landing(d).wait_recv()

        def drain():
            for d in range(1, n_narrow):
                copy(d).wait_send()

        return start, finish, drain

    face_start, face_finish, face_drain = gather(gather_faces, 0)
    source_start, source_finish, source_drain = gather(gather_source, 1)
    face_start()

    def neighbour_sum(level, e, x):
        _, Y = dims(level)
        p = iterates[level]
        step = 1 << level
        mid = pl.ds(PAD, Y)
        here = p[e, x + 1, mid, :]
        total = (
            face_x[level][x] * p[e, x, mid, :]
            + face_x[level][x + 1] * p[e, x + 2, mid, :]
        )
        total += face_yl[level][x] * p[e, x + 1, PAD - 1 : PAD - 1 + Y, :]
        total += face_yh[level][x] * p[e, x + 1, PAD + 1 : PAD + 1 + Y, :]
        total += face_zl[level][x] * z_low(here, step)
        total += face_zh[level][x] * z_high(here, step)
        return here, total

    def sweep(level, e, x):
        here, total = neighbour_sum(level, e, x)
        return KEEP * here + weight[level][x] * (source[level][x] + total)

    def produce(level, e, values_of):
        X, Y = dims(level)
        p = iterates[level]

        def plane(x, carry):
            v = values_of(x)
            p[e, x + 1, PAD : PAD + Y, :] = v
            sent_rows[level][e, 0, pl.ds(x, 1), :] = v[:1]
            sent_rows[level][e, 1, pl.ds(x, 1), :] = v[Y - 1 :]
            return carry

        lax.fori_loop(0, X, plane, 0, unroll=4)
        start, finish, drain = exchange(
            p.at[e],
            X,
            Y,
            sent_rows[level].at[e],
            got_rows[level].at[e],
            3 + 4 * level + e,
            order,
        )
        start()
        drains.append(drain)
        push()
        finish()

    for level in range(LEVELS):
        X, Y = dims(level)
        produce(level, 0, lambda x, level=level: weight[level][x] * source[level][x])
        produce(level, 1, lambda x, level=level: sweep(level, 0, x))

        def restrict(x, carry, level=level, Y=Y):
            both = None
            for k in range(2):
                here, total = neighbour_sum(level, 1, 2 * x + k)
                left = (source[level][2 * x + k] - diag[level][2 * x + k] * here) + total
                both = left if both is None else both + left
            tmp[:Y, :] = both
            half = Y // 2
            summed = (
                tmp[pl.ds(0, half, stride=2), :] + tmp[pl.ds(1, half, stride=2), :]
            )
            summed = 0.5 * z_pair(summed, level)
            if level + 1 == LEVELS:
                gather_source[narrow, x] = summed
            else:
                source[level + 1][x] = summed
            return carry

        if level + 1 == LEVELS:
            for x in range(X // 2):
                restrict(x, 0)
        else:
            lax.fori_loop(0, X // 2, restrict, 0, unroll=4)

    source_start()
    push()
    face_finish()
    source_finish()
    X, Y = dims(LEVELS)
    step = 1 << LEVELS
    row = lax.broadcasted_iota(jnp.int32, (Y, Z), 0)
    col = lax.broadcasted_iota(jnp.int32, (Y, Z), 1)
    for n in range(n_narrow):
        for x in range(X):
            fxl, fxh = gather_faces[n, x], gather_faces[n, x + 1]
            fyl, fyh, fzl, fzh = (gather_faces[n, X + 1 + k * X + x] for k in range(4))
            total = ((fxl + fxh) + (fyl + fyh)) + (fzl + fzh)
            w = DAMPING / total
            at = n * X + x
            coef[0, at] = w * fxl
            coef[1, at] = w * fxh
            coef[2, at] = jnp.where(row == 0, 0.0, w * fyl)
            coef[3, at] = jnp.where(row == Y - 1, 0.0, w * fyh)
            coef[4, at] = jnp.where(col < step, 0.0, w * fzl)
            coef[5, at] = jnp.where(col >= Z - step, 0.0, w * fzh)
            coef[6, at] = w * gather_source[n, x]

    zero_plane = jnp.zeros((1, Y, Z), jnp.float32)

    def bottom(k, cur):
        new = KEEP * cur + coef[6]
        new += coef[0] * jnp.concatenate([zero_plane, cur[:-1]], axis=0)
        new += coef[1] * jnp.concatenate([cur[1:], zero_plane], axis=0)
        new += coef[2] * pltpu.roll(cur, 1, 1)
        new += coef[3] * pltpu.roll(cur, Y - 1, 1)
        new += coef[4] * pltpu.roll(cur, step, 2)
        new += coef[5] * pltpu.roll(cur, Z - step, 2)
        return new

    coef[7] = lax.fori_loop(0, BOTTOM - 1, bottom, coef[6], unroll=15)
    for x in range(X):
        answer[LEVELS][x] = coef[7, narrow * X + x]

    for level in reversed(range(LEVELS)):
        X, Y = dims(level)
        half = Y // 2

        def raised(x, level=level, Y=Y, half=half):
            e = answer[level + 1][x // 2]
            tmp[pl.ds(0, half, stride=2), :] = e
            tmp[pl.ds(1, half, stride=2), :] = e
            return iterates[level][1, x + 1, PAD : PAD + Y, :] + tmp[:Y, :]

        produce(level, 2, raised)
        produce(level, 3, lambda x, level=level: sweep(level, 2, x))
        target = out_ref if level == 0 else answer[level]

        def close(x, carry, level=level, target=target):
            target[x] = sweep(level, 3, x)
            return carry

        lax.fori_loop(0, X, close, 0, unroll=4)

    assert len(pushed) == len(shares)

    def end(k, carry):
        carry_landing(k).wait_recv()
        carry_copy(k).wait_send()
        return carry

    lax.fori_loop(1, owners, end, 0)
    lax.fori_loop(1, owners, solved_end, 0)
    own_copy.wait()
    face_drain()
    source_drain()
    for drain in drains:
        drain()


def f32(*shape):
    return pltpu.VMEM(shape, jnp.float32)


def call_solve(n_wide, n_narrow, receive_index, solved, carried):
    X3, Y3 = dims(LEVELS)
    levels = [dims(level) for level in range(LEVELS)]
    padded = f32(X0 + 2, Y0 + 2 * PAD, Z)
    each = [f32(X, Y, Z) for X, Y in levels]
    moves = 3 + 4 * LEVELS
    scratch = [
        f32(64, Z),
        f32(Y0, Z),
        padded,
        padded,
        f32(X0, Y0, Z),
        padded,
        f32(2, 2, X0, Z),
        f32(2, 2, X0, Z),
        [f32(4, X + 2, Y + 2 * PAD, Z) for X, Y in levels],
        [f32(4, 2, X, Z) for X, Y in levels],
        [f32(4, 2, X, Z) for X, Y in levels],
        [f32(X + 1, Y, Z) for X, Y in levels],
        each,
        each,
        each,
        each,
        each,
        each,
        each,
        [f32(*dims(level), Z) for level in range(LEVELS + 1)],
        f32(n_narrow, 5 * X3 + 1, Y3, Z),
        f32(n_narrow, X3, Y3, Z),
        f32(8, n_narrow * X3, Y3, Z),
        pltpu.SemaphoreType.DMA((moves, 4)),
        pltpu.SemaphoreType.DMA((moves, 4)),
        pltpu.SemaphoreType.DMA((2, n_narrow - 1)),
        pltpu.SemaphoreType.DMA((2, n_narrow - 1)),
        pltpu.SemaphoreType.DMA((n_wide * n_narrow,)),
        pltpu.SemaphoreType.DMA((n_wide * n_narrow,)),
        pltpu.SemaphoreType.DMA((2,)),
        pltpu.SemaphoreType.DMA((n_wide * n_narrow,)),
        pltpu.SemaphoreType.DMA((n_wide * n_narrow,)),
    ]
    return pl.pallas_call(
        functools.partial(solve_kernel, n_wide, n_narrow),
        out_shape=(
            jax.ShapeDtypeStruct((X0, Y0, Z), jnp.float32),
            jax.ShapeDtypeStruct(solved.shape, solved.dtype),
            jax.ShapeDtypeStruct(carried.shape, carried.dtype),
        ),
        in_specs=[
            pl.BlockSpec(memory_space=pltpu.SMEM),
            pl.BlockSpec(memory_space=pl.ANY),
            pl.BlockSpec(memory_space=pl.ANY),
        ],
        out_specs=(
            pl.BlockSpec(memory_space=pltpu.VMEM),
            pl.BlockSpec(memory_space=pltpu.VMEM),
            pl.BlockSpec(memory_space=pl.ANY),
        ),
        scratch_shapes=scratch,
        compiler_params=pltpu.CompilerParams(
            collective_id=0, has_side_effects=True, vmem_limit_bytes=VMEM_LIMIT
        ),
        cost_estimate=pl.CostEstimate(
            flops=200_000_000, bytes_accessed=200_000_000, transcendentals=0
        ),
    )(receive_index, solved, carried)


def shards(n_wide, n_narrow, target_slot, fields):
    per_owner, n_fields, cells = fields.shape
    owners = n_wide * n_narrow
    me = lax.axis_index("wide") * n_narrow + lax.axis_index("narrow")
    slots = owners * CAPACITY
    place = jnp.arange(per_owner, dtype=jnp.int32)
    own_target = lax.dynamic_slice_in_dim(target_slot, me * per_owner, per_owner) // per_owner
    earlier = jnp.sum(
        (
            (own_target[:, None] == own_target[None, :]) & (place[:, None] > place[None, :])
        ).astype(jnp.int32),
        axis=1,
    )
    own_slot = own_target * CAPACITY + earlier
    slot_ids = jnp.arange(slots, dtype=jnp.int32)
    send_index = jnp.sum(
        jnp.where(own_slot[None, :] == slot_ids[:, None], place[None, :], 0), axis=1
    )
    table = target_slot.reshape(owners, per_owner)
    to_me = table // per_owner == me
    rank = jnp.sum(
        (to_me[:, None, :] & (place[None, :, None] > place[None, None, :])).astype(jnp.int32),
        axis=2,
    )
    row = jnp.arange(owners, dtype=jnp.int32)[:, None] * CAPACITY + rank
    receive_index = jnp.sum(
        jnp.where(
            target_slot[None, :] == (me * per_owner + place)[:, None], row.reshape(-1)[None, :], 0
        ),
        axis=1,
    )

    smem = pl.BlockSpec(memory_space=pltpu.SMEM)
    vmem = pl.BlockSpec(memory_space=pltpu.VMEM)
    params = pltpu.CompilerParams(vmem_limit_bytes=VMEM_LIMIT)
    carried_fields = n_fields - SOLVED
    solved, carried = pl.pallas_call(
        pack_kernel,
        out_shape=(
            jax.ShapeDtypeStruct((slots, SOLVED, cells), fields.dtype),
            jax.ShapeDtypeStruct((slots, carried_fields, cells), fields.dtype),
        ),
        in_specs=[smem, vmem],
        out_specs=(vmem, vmem),
        compiler_params=params,
    )(send_index, fields)
    pressure, solved, carried = call_solve(n_wide, n_narrow, receive_index, solved, carried)
    migrated = pl.pallas_call(
        merge_kernel,
        out_shape=jax.ShapeDtypeStruct(fields.shape, fields.dtype),
        in_specs=[smem, vmem, vmem],
        out_specs=vmem,
        compiler_params=params,
    )(receive_index, solved, carried)
    return migrated, pressure


def solution(mesh):
    body = functools.partial(shards, mesh.shape["wide"], mesh.shape["narrow"])
    in_specs = (P(), P(("wide", "narrow"), None, None))
    out_specs = (P(("wide", "narrow"), None, None), P("narrow", "wide", None))
    return jax.shard_map(body, mesh=mesh, in_specs=in_specs, out_specs=out_specs, check_vma=False)
```
